32 devices in a mesh: tensor: 8 (over y, x, core), expert: 4 (over z).
Axes of the slice: x: 2, y: 2, z: 4, core: 2. Of those that a mesh axis runs over, the one named last changes fastest.
Arguments:
- acts: bfloat16 [192, 3072], P('expert', 'tensor'), may hold values from -6 to 6
- grad_out: bfloat16 [192, 3072], P('expert', 'tensor'), may hold values from -6 to 6
- routing: int32 [192, 2], P('expert'), may hold values from 0 to 3, all different within a row; in each aligned block of 48 rows (0 to 47, 48 to 95, ...) at most 48 rows name the same one
- gates: float32 [192, 2], P('expert'), may hold values from 0.1 to 1
- w_gate: bfloat16 [4, 3072, 8192], P('expert', None, 'tensor'), may hold values from -0.109375 to 0.109375
- w_up: bfloat16 [4, 3072, 8192], P('expert', None, 'tensor'), may hold values from -0.109375 to 0.109375
- w_down: bfloat16 [4, 8192, 3072], P('expert', 'tensor'), may hold values from -0.0625 to 0.0625
Outputs:
- grad_gate: bfloat16 [4, 3072, 8192], P('expert', None, 'tensor')
- grad_up: bfloat16 [4, 3072, 8192], P('expert', None, 'tensor')
- grad_down: bfloat16 [4, 8192, 3072], P('expert', 'tensor')
- grad_acts: bfloat16 [192, 3072], P('expert', 'tensor')
The draws below stay inside these ranges and needn't reach their ends.
Inputs may be any that keep to these rules, and one draw needn't show every extreme that they name: `routing`: within the tokens of one owner group (aligned blocks of 48 rows) no expert is named more than 48 times, a bound that some block reaches; a token's two experts differ.
All inputs are finite; a program needn't handle non-finite values.
Results may differ from the reference program's by a relative error of at most 0.02.
Values may be sent and summed in bfloat16 or wider, within the bound.
No kernel may reach another device: no remote copies, remote signals or barrier semaphores. Data moves between devices by JAX's collectives and lax.ppermute only.
A program may use at most 128 MiB of HBM per device.

```python
import math
import jax
import jax.numpy as jnp
import numpy as np
from jax import lax

D = 3072
FF = 8192
TOK_DEV = 48
EXPERTS = 4
CAP = 48
SLOTS = 192
TOKENS = 192
N_EXPERT = 4


def level_of(key, shape, pieces, low, largest):
    def one(dim, shards_of):
        draws = jax.random.uniform(jax.random.fold_in(jax.random.fold_in(key, 6), dim), (shards_of,), jnp.float32, low / len(pieces), largest / len(pieces))
        return jnp.repeat(jnp.exp(draws), shape[dim] // shards_of).reshape((-1,) + (1,) * (len(shape) - dim - 1))

    loudness = one(*pieces[0])
    for cut in pieces[1:]:
        loudness = loudness * one(*cut)
    return loudness


def deal_out(own_key, own, number, rows, number_of, top, most, slope):
    ranking = jax.random.permutation(own_key, number_of)
    crowded, usual = portions_of(number_of, rows * top, most, slope, True), portions_of(number_of, rows * top, most, slope, False)
    places = jnp.arange(number_of)

    def named(sizes, turn):
        used = int((sizes > 0).sum())
        fixed = max(1, used // 4)
        passed = fixed + (places - fixed + turn * (used - fixed)) % max(1, number_of - fixed)
        return jnp.zeros((number_of,), jnp.int32).at[ranking[jnp.where(places < fixed, places, passed)]].set(jnp.asarray(sizes, jnp.int32))

    sizes = jnp.where(number % 4 == 0, named(crowded, number // 4), named(usual, number - number // 4 - 1))
    mixed = jax.random.permutation(jax.random.fold_in(own, 3), number_of)
    source_of, sink = mixed[0:number_of // 2 * 2:2], mixed[1:number_of // 2 * 2:2]
    room = jnp.minimum(sizes[source_of] - 1, most - sizes[sink]) // 2
    room = jnp.where((source_of == ranking[0]) | (sink == ranking[0]) | (sizes[sink] == 0), 0, jnp.maximum(room, 0))
    passed = jax.random.randint(jax.random.fold_in(own, 4), (number_of // 2,), 0, 1 << 20) % (room + 1)
    sizes = sizes.at[source_of].add(-passed).at[sink].add(passed)
    labels = jnp.searchsorted(jnp.cumsum(sizes), jnp.arange(rows * top), side="right").astype(jnp.int32)
    grid = labels.reshape(top, rows).T
    grid = grid[jax.random.permutation(jax.random.fold_in(own, 1), rows)]
    turn = jax.random.randint(jax.random.fold_in(own, 2), (rows, 1), 0, top)
    return jnp.take_along_axis(grid, (jnp.arange(top)[None, :] + turn) % top, axis=1)


def portions_of(amount, total, reach, skew, full):
    weights = [(1 << 20) // math.isqrt(grade ** skew) + 1 for grade in range(1, amount + 1)]
    largest = reach if full else min(reach, max(-(-total // amount), total * weights[0] // sum(weights)))
    least = 1 if total - largest >= amount - 1 else 0
    given, spare = [largest] + [least] * (amount - 1), total - largest - least * (amount - 1)
    while spare > 0:
        movable = [i for i in range(1, amount) if given[i] < largest] or [i for i in range(1, amount) if given[i] < reach]
        pool, remaining = sum([weights[i] for i in movable]), spare
        for i in movable:
            extra = min(reach - given[i], max(1, remaining * weights[i] // pool), spare)
            given[i] = given[i] + extra
            spare = spare - extra
    return np.array(given)


def normal_values(own_key, shape, deviation, limit, shards=(), kind=jnp.bfloat16):
    array = jax.random.normal(own_key, shape, jnp.float32) * deviation
    if len(shards) > 0:
        array = level_of(own_key, shape, shards, -0.22, 0.18) * array
    return jnp.clip(array, min=-limit, max=limit).astype(kind)


def setup_inputs(seed: int = 0) -> dict:
    arg_keys = jax.random.split(jax.random.key(seed), 8)
    acts = normal_values(arg_keys[0], (TOKENS, D), 1.0, 6.0, ((0, 4), (1, 8)))
    grad_out = normal_values(arg_keys[1], (TOKENS, D), 1.0, 6.0, ((0, 4), (1, 8)))
    routing_keys = jax.random.split(jax.random.fold_in(arg_keys[2], 1), TOKENS // TOK_DEV)
    routing_turns = jax.random.permutation(jax.random.fold_in(arg_keys[2], 3), TOKENS // TOK_DEV)
    routing = jax.vmap(lambda own, number: deal_out(jax.random.fold_in(arg_keys[2], 2), own, number, TOK_DEV, EXPERTS, 2, CAP, 2))(routing_keys, routing_turns).reshape((TOKENS, 2))
    gates = jnp.clip(0.1 + 0.9 * jax.random.uniform(arg_keys[3], (TOKENS, 2), jnp.float32) ** level_of(arg_keys[3], (TOKENS, 2), ((0, 4),), -0.2, 0.2), 0.1, 1.0)
    w_gate = normal_values(arg_keys[4], (EXPERTS, D, FF), D ** -0.5, 0.109375, ((0, 4), (2, 8)))
    w_up = normal_values(arg_keys[5], (EXPERTS, D, FF), D ** -0.5, 0.109375, ((0, 4), (2, 8)))
    w_down = normal_values(arg_keys[6], (EXPERTS, FF, D), FF ** -0.5, 0.0625, ((0, 4), (1, 8)))
    return {"acts": acts, "grad_out": grad_out, "routing": routing, "gates": gates, "w_gate": w_gate, "w_up": w_up, "w_down": w_down}


def dispatch_table(routing, gates, experts, capacity):
    tok_count = routing.shape[0]
    entries = routing.reshape(-1)
    chosen = (entries[:, None] == jnp.arange(experts, dtype=jnp.int32)[None, :]).astype(jnp.int32)
    earlier = jnp.cumsum(chosen, axis=0) - chosen
    position = jnp.sum(earlier * chosen, axis=1)
    in_slot = (position[:, None] == jnp.arange(capacity, dtype=jnp.int32)[None, :]).astype(jnp.float32)
    placed = chosen.astype(jnp.float32)[:, :, None] * in_slot[:, None, :]
    placed = placed.reshape(tok_count, 2, experts, capacity)
    table = jnp.sum(placed, axis=1)
    gate_slot = jnp.einsum("tkec,tk->ec", placed, gates.astype(jnp.float32))
    return table, gate_slot


def expert_backward(operands):
    rows_acts, rows_grad, gate_weight, up_weight, down_weight = operands
    gate_pre = jnp.dot(rows_acts, gate_weight, preferred_element_type=jnp.float32)
    up_pre = jnp.dot(rows_acts, up_weight, preferred_element_type=jnp.float32)
    gate_sig = jax.nn.sigmoid(gate_pre)
    gate_act = gate_pre * gate_sig
    hidden = (gate_act * up_pre).astype(jnp.bfloat16)
    grad_hidden = jnp.dot(rows_grad, down_weight.T, preferred_element_type=jnp.float32)
    grad_up_pre = (grad_hidden * gate_act).astype(jnp.bfloat16)
    grad_gate_pre = (grad_hidden * up_pre * gate_sig * (1.0 + gate_pre * (1.0 - gate_sig))).astype(jnp.bfloat16)
    grad_down = jnp.dot(hidden.T, rows_grad, preferred_element_type=jnp.float32).astype(jnp.bfloat16)
    grad_gate = jnp.dot(rows_acts.T, grad_gate_pre, preferred_element_type=jnp.float32).astype(jnp.bfloat16)
    grad_up = jnp.dot(rows_acts.T, grad_up_pre, preferred_element_type=jnp.float32).astype(jnp.bfloat16)
    slot_input = jnp.dot(grad_gate_pre, gate_weight.T, preferred_element_type=jnp.float32)
    slot_input = slot_input + jnp.dot(grad_up_pre, up_weight.T, preferred_element_type=jnp.float32)
    return grad_gate, grad_up, grad_down, slot_input.astype(jnp.bfloat16)


def group_table(group_routing, group_gates):
    return dispatch_table(group_routing, group_gates, EXPERTS, CAP)


def reference(acts, grad_out, routing, gates, w_gate, w_up, w_down):
    acts_group = acts.reshape(N_EXPERT, TOK_DEV, D).astype(jnp.float32)
    grad_group = grad_out.reshape(N_EXPERT, TOK_DEV, D).astype(jnp.float32)
    table, gate_slot = jax.vmap(group_table)(routing.reshape(N_EXPERT, TOK_DEV, 2), gates.reshape(N_EXPERT, TOK_DEV, 2))
    slot_acts = jnp.einsum("gtec,gtd->egcd", table, acts_group).astype(jnp.bfloat16)
    slot_grad = jnp.einsum("gtec,gtd->egcd", table, grad_group)
    slot_grad = (slot_grad * jnp.transpose(gate_slot, (1, 0, 2))[:, :, :, None]).astype(jnp.bfloat16)
    rows_acts = slot_acts.reshape(EXPERTS, SLOTS, D)
    rows_grad = slot_grad.reshape(EXPERTS, SLOTS, D)
    grad_gate, grad_up, grad_down, slot_input = lax.map(expert_backward, (rows_acts, rows_grad, w_gate, w_up, w_down))
    slot_input = slot_input.reshape(EXPERTS, N_EXPERT, CAP, D).astype(jnp.float32)
    grad_acts = jnp.einsum("gtec,egcd->gtd", table, slot_input).astype(jnp.bfloat16).reshape(TOKENS, D)
    return grad_gate, grad_up, grad_down, grad_acts
```

```python
import functools

import jax
import jax.numpy as jnp
from jax import lax
from jax.experimental import pallas as pl
from jax.experimental.pallas import tpu as pltpu
from jax.sharding import PartitionSpec as P

F32 = jnp.float32
BF16 = jnp.bfloat16
VMEM_LIMIT = 56 * 1024 * 1024


def dot(left, right, left_dim, right_dim):
    return lax.dot_general(
        left, right, (((left_dim,), (right_dim,)), ((), ())), preferred_element_type=F32
    )


def gate_of(routing, gates, expert):
    return jnp.sum(jnp.where(routing == expert, gates, 0.0), axis=1, keepdims=True)


def hidden_grads(gate_pre, up_pre, grad_hidden):
    sig = jax.nn.sigmoid(gate_pre)
    act = gate_pre * sig
    hidden = (act * up_pre).astype(BF16)
    grad_up_pre = (grad_hidden * act).astype(BF16)
    grad_gate_pre = (grad_hidden * up_pre * sig * (1.0 + gate_pre * (1.0 - sig))).astype(BF16)
    return hidden, grad_gate_pre, grad_up_pre


def middle_kernel(place, *refs):
    own, sib = refs[0:4], refs[4:8]
    wg, wu, wd = refs[8:11]
    x_out, g_out, hid, dg, du, keep, send = refs[11:18]
    wgv, wuv, wdv, sems = refs[18:22]
    chip, core = place[0] // 2, place[0] % 2
    width = own[0].shape[2]
    wide = 2 * width
    hidden_count = wgv.shape[1]
    step = 256
    chunks = hidden_count // step
    copies = []
    for f in range(chunks):
        group = []
        cols = pl.ds(f * step, step)
        for p in range(4):
            rows = pl.ds(pl.multiple_of((chip ^ p) * wide, wide), wide)
            here = pl.ds(p * wide, wide)
            group.append(pltpu.make_async_copy(wg.at[rows, cols], wgv.at[here, cols], sems.at[f, p]))
            group.append(pltpu.make_async_copy(wu.at[rows, cols], wuv.at[here, cols], sems.at[f, 4 + p]))
            group.append(pltpu.make_async_copy(wd.at[cols, rows], wdv.at[cols, here], sems.at[f, 8 + p]))
        for copy in group:
            copy.start()
        copies.append(group)
    first = core == 0
    for p in range(4):
        for array, out in ((0, x_out), (1, g_out)):
            mine, other = own[p][array], sib[p][array]
            out[:, p * wide : p * wide + width] = jnp.where(first, mine, other)
            out[:, p * wide + width : (p + 1) * wide] = jnp.where(first, other, mine)
    for f in range(chunks):
        cols = slice(f * step, (f + 1) * step)
        for copy in copies[f]:
            copy.wait()
        gate_pre = dot(x_out[...], wgv[:, cols], 1, 0)
        up_pre = dot(x_out[...], wuv[:, cols], 1, 0)
        grad_hidden = dot(g_out[...], wdv[cols, :], 1, 1)
        hid[:, cols], dg[:, cols], du[:, cols] = hidden_grads(gate_pre, up_pre, grad_hidden)
    for p in (3, 1, 2, 0):
        rows = slice(p * wide, (p + 1) * wide)
        part = dot(dg[...], wgv[rows, :], 1, 1) + dot(du[...], wuv[rows, :], 1, 1)
        low, high = part[:, :width], part[:, width:]
        keep[p] = jnp.where(first, low, high)
        send[p] = jnp.where(first, high, low).astype(BF16)


def middle(place, own, sib, wg, wu, wd):
    rows, width = own[0].shape[1:]
    full, hidden_count = wg.shape
    vmem = pl.BlockSpec(memory_space=pltpu.VMEM)
    hbm = pl.BlockSpec(memory_space=pl.ANY)
    shape = jax.ShapeDtypeStruct
    flops = 2 * rows * full * hidden_count * 5
    return pl.pallas_call(
        middle_kernel,
        out_shape=(
            shape((rows, full), BF16),
            shape((rows, full), BF16),
            shape((rows, hidden_count), BF16),
            shape((rows, hidden_count), BF16),
            shape((rows, hidden_count), BF16),
            shape((4, rows, width), F32),
            shape((4, rows, width), BF16),
        ),
        in_specs=[pl.BlockSpec(memory_space=pltpu.SMEM)] + [vmem] * 8 + [hbm] * 3,
        out_specs=[vmem] * 7,
        scratch_shapes=[
            pltpu.VMEM((full, hidden_count), BF16),
            pltpu.VMEM((full, hidden_count), BF16),
            pltpu.VMEM((hidden_count, full), BF16),
            pltpu.SemaphoreType.DMA((hidden_count // 256, 12)),
        ],
        compiler_params=pltpu.CompilerParams(vmem_limit_bytes=VMEM_LIMIT),
        cost_estimate=pl.CostEstimate(
            flops=flops, bytes_accessed=6 * full * hidden_count, transcendentals=rows * hidden_count
        ),
    )(place, *own, *sib, wg, wu, wd)


def rows_kernel(place, x, d, out):
    out[...] = dot(x[...], d[...], 0, 0).astype(BF16)


def grad_in(place, x, d):
    rows, full = x.shape
    hidden_count = d.shape[1]
    wide = full // 4
    return pl.pallas_call(
        rows_kernel,
        out_shape=jax.ShapeDtypeStruct((full, hidden_count), BF16),
        grid_spec=pltpu.PrefetchScalarGridSpec(
            num_scalar_prefetch=1,
            grid=(4,),
            in_specs=[
                pl.BlockSpec((rows, wide), lambda p, place: (0, p)),
                pl.BlockSpec((rows, hidden_count), lambda p, place: (0, 0)),
            ],
            out_specs=pl.BlockSpec((wide, hidden_count), lambda p, place: ((place[0] // 2) ^ p, 0)),
        ),
        compiler_params=pltpu.CompilerParams(vmem_limit_bytes=VMEM_LIMIT),
        cost_estimate=pl.CostEstimate(
            flops=2 * rows * full * hidden_count, bytes_accessed=2 * full * hidden_count, transcendentals=0
        ),
    )(place, x, d)


def grad_out_of(place, h, g):
    rows, full = g.shape
    hidden_count = h.shape[1]
    wide = full // 4
    return pl.pallas_call(
        rows_kernel,
        out_shape=jax.ShapeDtypeStruct((hidden_count, full), BF16),
        grid_spec=pltpu.PrefetchScalarGridSpec(
            num_scalar_prefetch=1,
            grid=(4,),
            in_specs=[
                pl.BlockSpec((rows, hidden_count), lambda p, place: (0, 0)),
                pl.BlockSpec((rows, wide), lambda p, place: (0, p)),
            ],
            out_specs=pl.BlockSpec((hidden_count, wide), lambda p, place: (0, (place[0] // 2) ^ p)),
        ),
        compiler_params=pltpu.CompilerParams(vmem_limit_bytes=VMEM_LIMIT),
        cost_estimate=pl.CostEstimate(
            flops=2 * rows * full * hidden_count, bytes_accessed=2 * full * hidden_count, transcendentals=0
        ),
    )(place, h, g)


def across(array, mask):
    return lax.ppermute(array, "tensor", [(i, i ^ mask) for i in range(8)])


def along(array, distance, count):
    return lax.ppermute(array, "expert", [(i, (i + distance) % count) for i in range(count)])


def chips_body(acts, grad_out, routing, gates, w_gate, w_up, w_down):
    groups = lax.axis_size("expert")
    z = lax.axis_index("expert")
    place = lax.axis_index("tensor").astype(jnp.int32)[None]
    tok_count, width = acts.shape
    grad_wide = grad_out.astype(F32)

    def for_expert(distance):
        gate = gate_of(routing, gates, (z + distance) % groups)
        return jnp.stack([acts, (grad_wide * gate).astype(BF16)])

    blocks = [for_expert(0)] + [along(for_expert(k), k, groups) for k in range(1, groups)]
    own_piece = jnp.concatenate(blocks, axis=1)
    own = [own_piece] + [across(own_piece, 2 * p) for p in range(1, 4)]
    sib = [across(piece, 1) for piece in own]
    wg, wu, wd = w_gate[0], w_up[0], w_down[0]
    x_all, g_all, hid, dg, du, keep, send = middle(place, own, sib, wg, wu, wd)
    from_core = across(send, 1)
    grad_gate = grad_in(place, x_all, dg)
    grad_up = grad_in(place, x_all, du)
    grad_down = grad_out_of(place, hid, g_all)
    total = keep + from_core.astype(F32)
    parts = total[1:].astype(BF16)
    mine = total[0]
    for p in range(1, 4):
        mine = mine + across(parts[p - 1], 2 * p).astype(F32)
    mine = mine.reshape(groups, tok_count, width)
    back = mine[0]
    sent = mine.astype(BF16)
    for k in range(1, groups):
        back = back + along(sent[k], -k, groups).astype(F32)
    return (grad_gate[None], grad_up[None], grad_down[None], back.astype(BF16))


def any_body(acts, grad_out, routing, gates, w_gate, w_up, w_down):
    expert = lax.axis_index("expert")
    acts_all, grad_all = (
        lax.all_gather(
            lax.all_gather(array, "tensor", axis=1, tiled=True), "expert", axis=0, tiled=True
        )
        for array in (acts, grad_out)
    )
    routing_all = lax.all_gather(routing, "expert", axis=0, tiled=True)
    gates_all = lax.all_gather(gates, "expert", axis=0, tiled=True)
    grad_all = (grad_all.astype(F32) * gate_of(routing_all, gates_all, expert)).astype(BF16)
    wg, wu, wd = w_gate[0], w_up[0], w_down[0]
    hid, dg, du = hidden_grads(dot(acts_all, wg, 1, 0), dot(acts_all, wu, 1, 0), dot(grad_all, wd, 1, 1))
    partial = dot(dg, wg, 1, 1) + dot(du, wu, 1, 1)
    partial = lax.psum_scatter(partial, "tensor", scatter_dimension=1, tiled=True)
    back = lax.psum_scatter(partial, "expert", scatter_dimension=0, tiled=True)
    return (
        dot(acts_all, dg, 0, 0).astype(BF16)[None],
        dot(acts_all, du, 0, 0).astype(BF16)[None],
        dot(hid, grad_all, 0, 0).astype(BF16)[None],
        back.astype(BF16),
    )


def solution(mesh):
    chips = mesh.shape["tensor"] == 8
    return jax.shard_map(
        chips_body if chips else any_body,
        mesh=mesh,
        in_specs=(
            P("expert", "tensor"),
            P("expert", "tensor"),
            P("expert", None),
            P("expert", None),
            P("expert", None, "tensor"),
            P("expert", None, "tensor"),
            P("expert", "tensor", None),
        ),
        out_specs=(
            P("expert", None, "tensor"),
            P("expert", None, "tensor"),
            P("expert", "tensor", None),
            P("expert", "tensor"),
        ),
        check_vma=False,
    )
```

```python
import functools

import jax
import jax.numpy as jnp
from jax import lax
from jax.experimental import pallas as pl
from jax.experimental.pallas import tpu as pltpu
from jax.sharding import PartitionSpec as P

F32 = jnp.float32
BF16 = jnp.bfloat16


def dot(left, right, left_dim, right_dim):
    return lax.dot_general(
        left, right, (((left_dim,), (right_dim,)), ((), ())), preferred_element_type=F32
    )


def gate_of(routing, gates, expert):
    return jnp.sum(jnp.where(routing == expert, gates, 0.0), axis=1, keepdims=True)


def hidden_grads(gate_pre, up_pre, grad_hidden):
    sig = jax.nn.sigmoid(gate_pre)
    act = gate_pre * sig
    hidden = (act * up_pre).astype(BF16)
    grad_up_pre = (grad_hidden * act).astype(BF16)
    grad_gate_pre = (grad_hidden * up_pre * sig * (1.0 + gate_pre * (1.0 - sig))).astype(BF16)
    return hidden, grad_gate_pre, grad_up_pre


VMEM = pl.BlockSpec(memory_space=pltpu.VMEM)
SMEM = pl.BlockSpec(memory_space=pltpu.SMEM)
HBM = pl.BlockSpec(memory_space=pl.ANY)


def shape(dims, dtype):
    return jax.ShapeDtypeStruct(dims, dtype)


def call(kernel, out_shape, in_specs, out_specs, flops, moved, scratch=(), limit=16, aliases={}):
    return pl.pallas_call(
        kernel,
        out_shape=out_shape,
        in_specs=in_specs,
        out_specs=out_specs,
        scratch_shapes=scratch,
        input_output_aliases=aliases,
        compiler_params=pltpu.CompilerParams(vmem_limit_bytes=limit * 1024 * 1024),
        cost_estimate=pl.CostEstimate(flops=flops, bytes_accessed=moved, transcendentals=0),
    )


def both_cores(core, mine, other):
    first = core == 0
    return jnp.concatenate([jnp.where(first, mine, other), jnp.where(first, other, mine)], axis=1)


def block_at(place, p, wide):
    return pl.ds(pl.multiple_of((place[0] // 2 ^ p) * wide, wide), wide)


STEP = 256
LOAD_LIMIT = 28


def half_at(place, m, width):
    return pl.ds(pl.multiple_of((place[0] ^ m) * width, width), width)


def pair(place, p, own, sib):
    core = place[0] % 2
    rows = block_at(place, p, 2 * own.shape[2])
    return rows, both_cores(core, own[0], sib[0]), both_cores(core, own[1], sib[1])


def half(place, m, ref):
    return half_at(place, m, ref.shape[2]), ref[0], ref[1]


def add_pieces(pieces, weights, acc_in, acc_out, finish, arrived=None):
    wg, wu, wd = weights
    for f in range(wg.shape[1] // STEP):
        cols = pl.ds(f * STEP, STEP)
        if arrived is not None:
            arrived(f)
        sums = [None if acc is None else acc[:, cols] for acc in acc_in]
        for rows, x, g in pieces:
            terms = (dot(x, wg[rows, cols], 1, 0), dot(x, wu[rows, cols], 1, 0), dot(g, wd[cols, rows], 1, 1))
            sums = [t if s is None else s + t for s, t in zip(sums, terms)]
        finish(cols, sums, acc_out)


def store(cols, sums, outs):
    for out, value in zip(outs, sums):
        out[:, cols] = value


def store_grads(cols, sums, outs):
    store(cols, hidden_grads(*sums), outs)


def load_kernel(place, own, wg, wu, wd, wg_here, wu_here, wd_here, gate, up, back, sems):
    copies = []
    for f in range(wg.shape[1] // STEP):
        cols = pl.ds(f * STEP, STEP)
        copies.append(
            [
                pltpu.make_async_copy(wg.at[:, cols], wg_here.at[:, cols], sems.at[f, 0]),
                pltpu.make_async_copy(wu.at[:, cols], wu_here.at[:, cols], sems.at[f, 1]),
                pltpu.make_async_copy(wd.at[cols, :], wd_here.at[cols, :], sems.at[f, 2]),
            ]
        )
        for copy in copies[f]:
            copy.start()

    def arrived(f):
        for copy in copies[f]:
            copy.wait()

    weights = (wg_here, wu_here, wd_here)
    add_pieces([half(place, 0, own)], weights, (None,) * 3, (gate, up, back), store, arrived)


def load_weights(place, own, weights):
    rows, hidden_count = own.shape[1], weights[0].shape[1]
    return call(
        load_kernel,
        tuple(shape(w.shape, BF16) for w in weights) + (shape((rows, hidden_count), F32),) * 3,
        [SMEM] + [VMEM] + [HBM] * 3,
        [VMEM] * 6,
        1,
        1,
        scratch=[pltpu.SemaphoreType.DMA((hidden_count // STEP, 3))],
        limit=LOAD_LIMIT,
    )(place, own, *weights)


def partial_kernel(place, near, own, sib, wg, wu, wd, *refs):
    pieces = [half(place, 1, near), pair(place, 3, own, sib)]
    add_pieces(pieces, (wg, wu, wd), refs[:3], refs[3:], store)


def partial_sums(place, near, own, sib, weights, acc):
    rows, hidden_count = own.shape[1], weights[0].shape[1]
    return call(
        partial_kernel,
        (shape((rows, hidden_count), F32),) * 3,
        [SMEM] + [VMEM] * 9,
        [VMEM] * 3,
        1,
        1,
        aliases={7: 0, 8: 1, 9: 2},
    )(place, near, own, sib, *weights, *acc)


def slot_rows(place, p, dg, du, wg, wu, wide):
    rows = block_at(place, p, wide)
    return dot(dg, wg[rows, :], 1, 1) + dot(du, wu[rows, :], 1, 1)


def middle_kernel(pieces, order, place, *refs):
    n = len(pieces)
    own, sib = refs[:n], refs[n : 2 * n]
    wg, wu, wd = refs[2 * n : 2 * n + 3]
    acc = refs[2 * n + 3 : 2 * n + 6]
    hid, dg, du, keep, send = refs[2 * n + 6 :]
    halves = [pair(place, p, o, s) for p, o, s in zip(pieces, own, sib)]
    add_pieces(halves, (wg, wu, wd), acc, (hid, dg, du), store_grads)
    width = own[0].shape[2]
    first = place[0] % 2 == 0
    for p in order:
        part = slot_rows(place, p, dg[...], du[...], wg, wu, 2 * width)
        low, high = part[:, :width], part[:, width:]
        keep[p - 1] = jnp.where(first, low, high)
        send[p - 1] = jnp.where(first, high, low).astype(BF16)


def middle(place, pieces, own, sib, weights, acc):
    rows, width = own[0].shape[1:]
    hidden_count = weights[0].shape[1]
    return call(
        functools.partial(middle_kernel, pieces, (3, 1, 2)),
        (shape((rows, hidden_count), BF16),) * 3
        + (shape((3, rows, width), F32), shape((3, rows, width), BF16)),
        [SMEM] + [VMEM] * (2 * len(pieces) + 6),
        [VMEM] * 5,
        24 * rows * width * hidden_count * 2,
        0,
    )(place, *own, *sib, *weights, *acc)


def own_slot_kernel(place, dg, du, wg, wu, keep, send):
    width = keep.shape[1]
    first = place[0] % 2 == 0
    part = slot_rows(place, 0, dg[...], du[...], wg, wu, 2 * width)
    low, high = part[:, :width], part[:, width:]
    keep[...] = jnp.where(first, low, high)
    send[...] = jnp.where(first, high, low).astype(BF16)


def own_slot(place, dg, du, wg, wu):
    rows, hidden_count = dg.shape
    width = wg.shape[0] // 8
    return call(
        own_slot_kernel,
        (shape((rows, width), F32), shape((rows, width), BF16)),
        [SMEM] + [VMEM] * 4,
        [VMEM] * 2,
        8 * rows * width * hidden_count,
        0,
    )(place, dg, du, wg, wu)


def weight_kernel(array, place, *refs):
    own, sib, d, out, buf, sems = refs[0:4], refs[4:8], refs[8], refs[9], refs[10], refs[11]
    core = place[0] % 2
    wide = 2 * own[0].shape[2]
    copies = []
    for p in range(4):
        rows = block_at(place, p, wide)
        piece = both_cores(core, own[p][array], sib[p][array])
        if array == 0:
            buf[p] = dot(piece, d[...], 0, 0).astype(BF16)
            target = out.at[rows, :]
        else:
            buf[p] = dot(d[...], piece, 0, 0).astype(BF16)
            target = out.at[:, rows]
        copies.append(pltpu.make_async_copy(buf.at[p], target, sems.at[p]))
        copies[p].start()
    for copy in copies:
        copy.wait()


def weight_grad(place, array, own, sib, d):
    rows, width = own[0].shape[1:]
    hidden_count = d.shape[1]
    block = (2 * width, hidden_count) if array == 0 else (hidden_count, 2 * width)
    out = (8 * width, hidden_count) if array == 0 else (hidden_count, 8 * width)
    return call(
        functools.partial(weight_kernel, array),
        shape(out, BF16),
        [SMEM] + [VMEM] * 9,
        HBM,
        16 * rows * width * hidden_count,
        16 * width * hidden_count,
        scratch=[pltpu.VMEM((4,) + block, BF16), pltpu.SemaphoreType.DMA((4,))],
    )(place, *own, *sib, d)


def across(array, mask):
    return lax.ppermute(array, "tensor", [(i, i ^ mask) for i in range(8)])


def along(array, distance, count):
    return lax.ppermute(array, "expert", [(i, (i + distance) % count) for i in range(count)])


def chips_body(acts, grad_out, routing, gates, w_gate, w_up, w_down):
    groups = lax.axis_size("expert")
    z = lax.axis_index("expert")
    place = lax.axis_index("tensor").astype(jnp.int32)[None]
    tok_count, width = acts.shape
    grad_wide = grad_out.astype(F32)

    def for_expert(distance):
        gate = gate_of(routing, gates, (z + distance) % groups)
        return jnp.stack([acts, (grad_wide * gate).astype(BF16)])

    blocks = [for_expert(0)] + [along(for_expert(k), k, groups) for k in range(1, groups)]
    own_piece = jnp.concatenate(blocks, axis=1)
    own = [own_piece] + [across(own_piece, 2 * p) for p in range(1, 4)]
    near = across(own[0], 1)
    weights = (w_gate[0], w_up[0], w_down[0])
    loaded = load_weights(place, own[0], weights)
    weights, acc = loaded[:3], loaded[3:]
    *own[1:], acc = lax.optimization_barrier((*own[1:], acc))
    sib = [near] + [across(piece, 1) for piece in own[1:]]
    acc = partial_sums(place, near, own[3], sib[3], weights, acc)
    hid, dg, du, keep, send = middle(place, (1, 2), own[1:3], sib[1:3], weights, acc)
    from_core = across(send, 1)
    keep_own, send_own = own_slot(place, dg, du, *weights[:2])
    own_from_core = across(send_own, 1)
    grad_gate = weight_grad(place, 0, own, sib, dg)
    grad_up = weight_grad(place, 0, own, sib, du)
    grad_down = weight_grad(place, 1, own, sib, hid)
    parts = (keep + from_core.astype(F32)).astype(BF16)
    mine = keep_own + own_from_core.astype(F32)
    for p in range(1, 4):
        mine = mine + across(parts[p - 1], 2 * p).astype(F32)
    mine = mine.reshape(groups, tok_count, width)
    back = mine[0]
    sent = mine.astype(BF16)
    for k in range(1, groups):
        back = back + along(sent[k], -k, groups).astype(F32)
    return (grad_gate[None], grad_up[None], grad_down[None], back.astype(BF16))


def any_body(acts, grad_out, routing, gates, w_gate, w_up, w_down):
    expert = lax.axis_index("expert")
    acts_all, grad_all = (
        lax.all_gather(
            lax.all_gather(array, "tensor", axis=1, tiled=True), "expert", axis=0, tiled=True
        )
        for array in (acts, grad_out)
    )
    routing_all = lax.all_gather(routing, "expert", axis=0, tiled=True)
    gates_all = lax.all_gather(gates, "expert", axis=0, tiled=True)
    grad_all = (grad_all.astype(F32) * gate_of(routing_all, gates_all, expert)).astype(BF16)
    wg, wu, wd = w_gate[0], w_up[0], w_down[0]
    hid, dg, du = hidden_grads(dot(acts_all, wg, 1, 0), dot(acts_all, wu, 1, 0), dot(grad_all, wd, 1, 1))
    partial = dot(dg, wg, 1, 1) + dot(du, wu, 1, 1)
    partial = lax.psum_scatter(partial, "tensor", scatter_dimension=1, tiled=True)
    back = lax.psum_scatter(partial, "expert", scatter_dimension=0, tiled=True)
    return (
        dot(acts_all, dg, 0, 0).astype(BF16)[None],
        dot(acts_all, du, 0, 0).astype(BF16)[None],
        dot(hid, grad_all, 0, 0).astype(BF16)[None],
        back.astype(BF16),
    )


def solution(mesh):
    chips = mesh.shape["tensor"] == 8
    return jax.shard_map(
        chips_body if chips else any_body,
        mesh=mesh,
        in_specs=(
            P("expert", "tensor"),
            P("expert", "tensor"),
            P("expert", None),
            P("expert", None),
            P("expert", None, "tensor"),
            P("expert", None, "tensor"),
            P("expert", "tensor", None),
        ),
        out_specs=(
            P("expert", None, "tensor"),
            P("expert", None, "tensor"),
            P("expert", "tensor", None),
            P("expert", "tensor"),
        ),
        check_vma=False,
    )
```

```python
import functools

import jax
import jax.numpy as jnp
from jax import lax
from jax.experimental import pallas as pl
from jax.experimental.pallas import tpu as pltpu
from jax.sharding import PartitionSpec as P

F32 = jnp.float32
BF16 = jnp.bfloat16


def dot(left, right, left_dim, right_dim):
    return lax.dot_general(
        left, right, (((left_dim,), (right_dim,)), ((), ())), preferred_element_type=F32
    )


def gate_of(routing, gates, expert):
    return jnp.sum(jnp.where(routing == expert, gates, 0.0), axis=1, keepdims=True)


def hidden_grads(gate_pre, up_pre, grad_hidden):
    sig = jax.nn.sigmoid(gate_pre)
    act = gate_pre * sig
    hidden = (act * up_pre).astype(BF16)
    grad_up_pre = (grad_hidden * act).astype(BF16)
    grad_gate_pre = (grad_hidden * up_pre * sig * (1.0 + gate_pre * (1.0 - sig))).astype(BF16)
    return hidden, grad_gate_pre, grad_up_pre


VMEM = pl.BlockSpec(memory_space=pltpu.VMEM)
SMEM = pl.BlockSpec(memory_space=pltpu.SMEM)
HBM = pl.BlockSpec(memory_space=pl.ANY)


def shape(dims, dtype):
    return jax.ShapeDtypeStruct(dims, dtype)


def call(kernel, out_shape, in_specs, out_specs, flops, moved, scratch=(), limit=16, aliases={}):
    return pl.pallas_call(
        kernel,
        out_shape=out_shape,
        in_specs=in_specs,
        out_specs=out_specs,
        scratch_shapes=scratch,
        input_output_aliases=aliases,
        compiler_params=pltpu.CompilerParams(vmem_limit_bytes=limit * 1024 * 1024),
        cost_estimate=pl.CostEstimate(flops=flops, bytes_accessed=moved, transcendentals=0),
    )


def both_cores(core, mine, other):
    first = core == 0
    return jnp.concatenate([jnp.where(first, mine, other), jnp.where(first, other, mine)], axis=1)


def block_at(place, p, wide):
    return pl.ds(pl.multiple_of((place[0] // 2 ^ p) * wide, wide), wide)


STEP = 256
LOAD_LIMIT = 28


def far(place):
    core = place[0] % 2
    return 0, 1 + core, 2 - core, 3


def pair(place, i, own, sib):
    core = place[0] % 2
    rows = block_at(place, far(place)[i], 2 * own.shape[2])
    return rows, both_cores(core, own[0], sib[0]), both_cores(core, own[1], sib[1])


def add_pieces(pieces, weights, acc_in, acc_out, finish, arrived=None):
    wg, wu, wd = weights
    for f in range(wg.shape[1] // STEP):
        cols = pl.ds(f * STEP, STEP)
        if arrived is not None:
            arrived(f)
        sums = [None if acc is None else acc[:, cols] for acc in acc_in]
        for rows, x, g in pieces:
            terms = (dot(x, wg[rows, cols], 1, 0), dot(x, wu[rows, cols], 1, 0), dot(g, wd[cols, rows], 1, 1))
            sums = [t if s is None else s + t for s, t in zip(sums, terms)]
        finish(cols, sums, acc_out)


def store(cols, sums, outs):
    for out, value in zip(outs, sums):
        out[:, cols] = value


def store_grads(cols, sums, outs):
    store(cols, hidden_grads(*sums), outs)


def load_kernel(place, own, near, wg, wu, wd, wg_here, wu_here, wd_here, gate, up, back, sems):
    copies = []
    for f in range(wg.shape[1] // STEP):
        cols = pl.ds(f * STEP, STEP)
        copies.append(
            [
                pltpu.make_async_copy(wg.at[:, cols], wg_here.at[:, cols], sems.at[f, 0]),
                pltpu.make_async_copy(wu.at[:, cols], wu_here.at[:, cols], sems.at[f, 1]),
                pltpu.make_async_copy(wd.at[cols, :], wd_here.at[cols, :], sems.at[f, 2]),
            ]
        )
        for copy in copies[f]:
            copy.start()

    def arrived(f):
        for copy in copies[f]:
            copy.wait()

    weights = (wg_here, wu_here, wd_here)
    add_pieces([pair(place, 0, own, near)], weights, (None,) * 3, (gate, up, back), store, arrived)


def load_weights(place, own, near, weights):
    rows, hidden_count = own.shape[1], weights[0].shape[1]
    return call(
        load_kernel,
        tuple(shape(w.shape, BF16) for w in weights) + (shape((rows, hidden_count), F32),) * 3,
        [SMEM] + [VMEM] * 2 + [HBM] * 3,
        [VMEM] * 6,
        1,
        1,
        scratch=[pltpu.SemaphoreType.DMA((hidden_count // STEP, 3))],
        limit=LOAD_LIMIT,
    )(place, own, near, *weights)


def partial_kernel(place, *refs):
    pieces = [pair(place, 1, *refs[0:2]), pair(place, 2, *refs[2:4])]
    add_pieces(pieces, refs[4:7], refs[7:10], refs[10:], store)


def partial_sums(place, halves, weights, acc):
    rows, hidden_count = acc[0].shape
    return call(
        partial_kernel,
        (shape((rows, hidden_count), F32),) * 3,
        [SMEM] + [VMEM] * 10,
        [VMEM] * 3,
        1,
        1,
        aliases={8: 0, 9: 1, 10: 2},
    )(place, *halves, *weights, *acc)


def slot_rows(place, p, dg, du, wg, wu, wide):
    rows = block_at(place, p, wide)
    return dot(dg, wg[rows, :], 1, 1) + dot(du, wu[rows, :], 1, 1)


def write_slots(place, p, dg, du, wg, wu, keep, send):
    width = keep.shape[1]
    first = place[0] % 2 == 0
    part = slot_rows(place, p, dg[...], du[...], wg, wu, 2 * width)
    low, high = part[:, :width], part[:, width:]
    keep[...] = jnp.where(first, low, high)
    send[...] = jnp.where(first, high, low).astype(BF16)


def middle_kernel(place, own, sib, wg, wu, wd, *refs):
    acc = refs[:3]
    hid, dg, du, keep, send = refs[3:]
    add_pieces([pair(place, 3, own, sib)], (wg, wu, wd), acc, (hid, dg, du), store_grads)
    write_slots(place, 3, dg, du, wg, wu, keep, send)


def middle(place, own, sib, weights, acc):
    rows, width = own.shape[1:]
    hidden_count = weights[0].shape[1]
    return call(
        middle_kernel,
        (shape((rows, hidden_count), BF16),) * 3 + (shape((rows, width), F32), shape((rows, width), BF16)),
        [SMEM] + [VMEM] * 8,
        [VMEM] * 5,
        20 * rows * width * hidden_count,
        0,
    )(place, own, sib, *weights, *acc)


def slot_kernel(p, place, *refs):
    write_slots(place, p, *refs)


def slots(place, p, dg, du, wg, wu):
    rows, hidden_count = dg.shape
    width = wg.shape[0] // 8
    return call(
        functools.partial(slot_kernel, p),
        (shape((rows, width), F32), shape((rows, width), BF16)),
        [SMEM] + [VMEM] * 4,
        [VMEM] * 2,
        8 * rows * width * hidden_count,
        0,
    )(place, dg, du, wg, wu)


def weight_kernel(arrays, place, *refs):
    n = len(arrays)
    own, sib, ds = refs[0:4], refs[4:8], refs[8 : 8 + n]
    outs, bufs, sems = refs[8 + n : 8 + 2 * n], refs[8 + 2 * n : 8 + 3 * n], refs[8 + 3 * n]
    core = place[0] % 2
    wide = 2 * own[0].shape[2]
    copies = []
    for i, (array, d, out, buf) in enumerate(zip(arrays, ds, outs, bufs)):
        for j, p in enumerate(far(place)):
            rows = block_at(place, p, wide)
            piece = both_cores(core, own[j][array], sib[j][array])
            if array == 0:
                buf[j] = dot(piece, d[...], 0, 0).astype(BF16)
                target = out.at[rows, :]
            else:
                buf[j] = dot(d[...], piece, 0, 0).astype(BF16)
                target = out.at[:, rows]
            copies.append(pltpu.make_async_copy(buf.at[j], target, sems.at[i, j]))
            copies[-1].start()
    for copy in copies:
        copy.wait()


def weight_grads(place, arrays, own, sib, ds):
    rows, width = own[0].shape[1:]
    hidden_count = ds[0].shape[1]
    blocks = [(2 * width, hidden_count) if array == 0 else (hidden_count, 2 * width) for array in arrays]
    outs = [(8 * width, hidden_count) if array == 0 else (hidden_count, 8 * width) for array in arrays]
    return call(
        functools.partial(weight_kernel, arrays),
        tuple(shape(out, BF16) for out in outs),
        [SMEM] + [VMEM] * (8 + len(ds)),
        [HBM] * len(ds),
        16 * rows * width * hidden_count * len(ds),
        16 * width * hidden_count * len(ds),
        scratch=[pltpu.VMEM((4,) + block, BF16) for block in blocks] + [pltpu.SemaphoreType.DMA((len(ds), 4))],
        limit=LOAD_LIMIT,
    )(place, *own, *sib, *ds)


def pack_kernel(groups, place, *refs):
    sources, outs, here, sems = refs[:4], refs[4 : 4 + groups], refs[4 + groups : 8 + groups], refs[8 + groups]
    copies = [pltpu.make_async_copy(s, d, sems.at[i]) for i, (s, d) in enumerate(zip(sources, here))]
    for copy in copies:
        copy.start()
    for copy in copies:
        copy.wait()
    acts, grad, routing, gates = here
    wide = grad[...].astype(F32)
    for distance, out in enumerate(outs):
        expert = lax.rem(place[0] + distance, groups)
        gate = jnp.sum(jnp.where(routing[...] == expert, gates[...], 0.0), axis=0, keepdims=True)
        out[0] = acts[...]
        out[1] = (wide * gate.T).astype(BF16)


def pack(place, acts, grad, routing, gates, groups):
    sources = (acts, grad, routing.T, gates.T)
    return call(
        functools.partial(pack_kernel, groups),
        (shape((2,) + acts.shape, BF16),) * groups,
        [SMEM] + [HBM] * 4,
        [VMEM] * groups,
        1,
        1,
        scratch=[pltpu.VMEM(s.shape, s.dtype) for s in sources] + [pltpu.SemaphoreType.DMA((4,))],
        limit=63,
    )(place, *sources)


def across(array, even, odd=None):
    masks = (even, even if odd is None else odd)
    return lax.ppermute(array, "tensor", [(i, i ^ masks[i % 2]) for i in range(8)])


def along(array, distance, count):
    return lax.ppermute(array, "expert", [(i, (i + distance) % count) for i in range(count)])


def chips_body(acts, grad_out, routing, gates, w_gate, w_up, w_down):
    groups = lax.axis_size("expert")
    place = lax.axis_index("tensor").astype(jnp.int32)[None]
    z = lax.axis_index("expert").astype(jnp.int32)[None]
    tok_count, width = acts.shape
    packed = pack(z, acts, grad_out, routing, gates, groups)
    blocks = [packed[0]] + [along(packed[k], k, groups) for k in range(1, groups)]
    own = jnp.concatenate(blocks, axis=1)
    near = across(own, 1)
    here = across(own, 2, 4), across(near, 2, 4)
    weights = (w_gate[0], w_up[0], w_down[0])
    loaded = load_weights(place, own, near, weights)
    weights, acc = loaded[:3], loaded[3:]
    here, acc = lax.optimization_barrier((here, acc))
    diag = across(here[0], 4, 2)
    there = across(here[1], 1), across(here[0], 1)
    acc = partial_sums(place, here + there, weights, acc)
    diag, acc = lax.optimization_barrier((diag, acc))
    diag_near = across(diag, 1)
    hid, dg, du, keep, send = middle(place, diag, diag_near, weights, acc)
    mine_of = own, here[0], there[0], diag
    other_of = near, here[1], there[1], diag_near
    wg, wu = weights[:2]

    def chip_sum(keep, send):
        return keep + across(send, 1).astype(F32)

    share = slots(place, 1, dg, du, wg, wu)
    diagonal, dg, du = lax.optimization_barrier((chip_sum(keep, send), dg, du))
    parts = [across(diagonal.astype(BF16), 6)]
    for p in (1, 2):
        later = slots(place, (p + 1) % 3, dg, du, wg, wu)
        total, dg, du = lax.optimization_barrier((chip_sum(*share), dg, du))
        parts.append(across(total.astype(BF16), 2 * p))
        share = later
    mine = chip_sum(*share)
    parts[0], dg = lax.optimization_barrier((parts[0], dg))
    (grad_gate,) = weight_grads(place, (0,), mine_of, other_of, (dg,))
    for part in parts:
        mine = mine + part.astype(F32)
    mine, du, hid = lax.optimization_barrier((mine, du, hid))
    grad_up, grad_down = weight_grads(place, (0, 1), mine_of, other_of, (du, hid))
    mine = mine.reshape(groups, tok_count, width)
    back = mine[0]
    sent = mine.astype(BF16)
    for k in range(1, groups):
        back = back + along(sent[k], -k, groups).astype(F32)
    return (grad_gate[None], grad_up[None], grad_down[None], back.astype(BF16))


def any_body(acts, grad_out, routing, gates, w_gate, w_up, w_down):
    expert = lax.axis_index("expert")
    acts_all, grad_all = (
        lax.all_gather(
            lax.all_gather(array, "tensor", axis=1, tiled=True), "expert", axis=0, tiled=True
        )
        for array in (acts, grad_out)
    )
    routing_all = lax.all_gather(routing, "expert", axis=0, tiled=True)
    gates_all = lax.all_gather(gates, "expert", axis=0, tiled=True)
    grad_all = (grad_all.astype(F32) * gate_of(routing_all, gates_all, expert)).astype(BF16)
    wg, wu, wd = w_gate[0], w_up[0], w_down[0]
    hid, dg, du = hidden_grads(dot(acts_all, wg, 1, 0), dot(acts_all, wu, 1, 0), dot(grad_all, wd, 1, 1))
    partial = dot(dg, wg, 1, 1) + dot(du, wu, 1, 1)
    partial = lax.psum_scatter(partial, "tensor", scatter_dimension=1, tiled=True)
    back = lax.psum_scatter(partial, "expert", scatter_dimension=0, tiled=True)
    return (
        dot(acts_all, dg, 0, 0).astype(BF16)[None],
        dot(acts_all, du, 0, 0).astype(BF16)[None],
        dot(hid, grad_all, 0, 0).astype(BF16)[None],
        back.astype(BF16),
    )


def solution(mesh):
    chips = mesh.shape["tensor"] == 8
    return jax.shard_map(
        chips_body if chips else any_body,
        mesh=mesh,
        in_specs=(
            P("expert", "tensor"),
            P("expert", "tensor"),
            P("expert", None),
            P("expert", None),
            P("expert", None, "tensor"),
            P("expert", None, "tensor"),
            P("expert", "tensor", None),
        ),
        out_specs=(
            P("expert", None, "tensor"),
            P("expert", None, "tensor"),
            P("expert", "tensor", None),
            P("expert", "tensor"),
        ),
        check_vma=False,
    )
```

```python
import functools

import jax
import jax.numpy as jnp
from jax import lax
from jax.experimental import pallas as pl
from jax.experimental.pallas import tpu as pltpu
from jax.sharding import PartitionSpec as P

F32 = jnp.float32
BF16 = jnp.bfloat16


def dot(left, right, left_dim, right_dim):
    return lax.dot_general(
        left, right, (((left_dim,), (right_dim,)), ((), ())), preferred_element_type=F32
    )


def gate_of(routing, gates, expert):
    return jnp.sum(jnp.where(routing == expert, gates, 0.0), axis=1, keepdims=True)


def hidden_grads(gate_pre, up_pre, grad_hidden):
    sig = jax.nn.sigmoid(gate_pre)
    act = gate_pre * sig
    hidden = (act * up_pre).astype(BF16)
    grad_up_pre = (grad_hidden * act).astype(BF16)
    grad_gate_pre = (grad_hidden * up_pre * sig * (1.0 + gate_pre * (1.0 - sig))).astype(BF16)
    return hidden, grad_gate_pre, grad_up_pre


VMEM = pl.BlockSpec(memory_space=pltpu.VMEM)
SMEM = pl.BlockSpec(memory_space=pltpu.SMEM)
HBM = pl.BlockSpec(memory_space=pl.ANY)


def shape(dims, dtype):
    return jax.ShapeDtypeStruct(dims, dtype)


def call(kernel, out_shape, in_specs, out_specs, flops, moved, scratch=(), limit=16, aliases={}):
    return pl.pallas_call(
        kernel,
        out_shape=out_shape,
        in_specs=in_specs,
        out_specs=out_specs,
        scratch_shapes=scratch,
        input_output_aliases=aliases,
        compiler_params=pltpu.CompilerParams(vmem_limit_bytes=limit * 1024 * 1024),
        cost_estimate=pl.CostEstimate(flops=flops, bytes_accessed=moved, transcendentals=0),
    )


def both_cores(core, mine, other):
    first = core == 0
    return jnp.concatenate([jnp.where(first, mine, other), jnp.where(first, other, mine)], axis=1)


def block_at(place, p, wide):
    return pl.ds(pl.multiple_of((place[0] // 2 ^ p) * wide, wide), wide)


STEP = 256
LOAD_LIMIT = 28
UP_FIRST, UP_LAST = (0,), (1, 2, 3)


def far(place):
    core = place[0] % 2
    return 0, 1 + core, 2 - core, 3


def pair(place, i, own, sib):
    core = place[0] % 2
    rows = block_at(place, far(place)[i], 2 * own.shape[2])
    return rows, both_cores(core, own[0], sib[0]), both_cores(core, own[1], sib[1])


def add_pieces(pieces, weights, acc_in, acc_out, finish):
    wg, wu, wd = weights
    for f in range(wg.shape[1] // STEP):
        cols = pl.ds(f * STEP, STEP)
        sums = [None if acc is None else acc[:, cols] for acc in acc_in]
        for rows, x, g in pieces:
            terms = (dot(x, wg[rows, cols], 1, 0), dot(x, wu[rows, cols], 1, 0), dot(g, wd[cols, rows], 1, 1))
            sums = [t if s is None else s + t for s, t in zip(sums, terms)]
        finish(cols, sums, acc_out)


def store(cols, sums, outs):
    for out, value in zip(outs, sums):
        out[:, cols] = value


def store_grads(cols, sums, outs):
    store(cols, hidden_grads(*sums), outs)


def load_kernel(place, own, near, *refs):
    sources, here, sums, sems = refs[:2], refs[2:4], refs[4:6], refs[6]
    row, x, _ = pair(place, 0, own, near)
    wide = x.shape[1]
    copies = []
    for p in range(4):
        rows = block_at(place, p, wide)
        for i, (s, h) in enumerate(zip(sources, here)):
            copies.append(pltpu.make_async_copy(s.at[rows, :], h.at[rows, :], sems.at[i, p]))
            copies[-1].start()
    for copy, weight, total in zip(copies, here, sums):
        copy.wait()
        for f in range(weight.shape[1] // STEP):
            cols = pl.ds(f * STEP, STEP)
            total[:, cols] = dot(x, weight[row, cols], 1, 0)
    for copy in copies[2:]:
        copy.wait()


def load(place, own, near, wg, wu):
    rows, hidden_count = own.shape[1], wg.shape[1]
    return call(
        load_kernel,
        (shape(wg.shape, BF16),) * 2 + (shape((rows, hidden_count), F32),) * 2,
        [SMEM] + [VMEM] * 2 + [HBM] * 2,
        [VMEM] * 4,
        1,
        1,
        scratch=[pltpu.SemaphoreType.DMA((2, 4))],
        limit=36,
    )(place, own, near, wg, wu)


def back_kernel(place, own, near, wd, back):
    row, _, g = pair(place, 0, own, near)
    for f in range(wd.shape[0] // STEP):
        cols = pl.ds(f * STEP, STEP)
        back[:, cols] = dot(g, wd[cols, row], 1, 1)


def own_back(place, own, near, wd):
    rows, hidden_count = own.shape[1], wd.shape[0]
    return call(
        back_kernel, shape((rows, hidden_count), F32), [SMEM] + [VMEM] * 3, VMEM, 1, 1
    )(place, own, near, wd)


def partial_kernel(i, place, own, sib, wg, wu, wd, *refs):
    add_pieces([pair(place, i, own, sib)], (wg, wu, wd), refs[:3], refs[3:], store)


def partial_sums(place, i, own, sib, weights, acc):
    rows, hidden_count = acc[0].shape
    return call(
        functools.partial(partial_kernel, i),
        (shape((rows, hidden_count), F32),) * 3,
        [SMEM] + [VMEM] * 8,
        [VMEM] * 3,
        1,
        1,
        aliases={6: 0, 7: 1, 8: 2},
    )(place, own, sib, *weights, *acc)


def slot_rows(place, p, dg, du, wg, wu, wide):
    rows = block_at(place, p, wide)
    return dot(dg, wg[rows, :], 1, 1) + dot(du, wu[rows, :], 1, 1)


def write_slots(place, p, dg, du, wg, wu, keep, send):
    width = keep.shape[1]
    first = place[0] % 2 == 0
    part = slot_rows(place, p, dg[...], du[...], wg, wu, 2 * width)
    low, high = part[:, :width], part[:, width:]
    keep[...] = jnp.where(first, low, high)
    send[...] = jnp.where(first, high, low).astype(BF16)


def middle_kernel(place, own, sib, wg, wu, wd, *refs):
    acc = refs[:3]
    hid, dg, du, keep, send = refs[3:]
    add_pieces([pair(place, 3, own, sib)], (wg, wu, wd), acc, (hid, dg, du), store_grads)
    write_slots(place, 3, dg, du, wg, wu, keep, send)


def middle(place, own, sib, weights, acc):
    rows, width = own.shape[1:]
    hidden_count = weights[0].shape[1]
    return call(
        middle_kernel,
        (shape((rows, hidden_count), BF16),) * 3 + (shape((rows, width), F32), shape((rows, width), BF16)),
        [SMEM] + [VMEM] * 8,
        [VMEM] * 5,
        20 * rows * width * hidden_count,
        0,
    )(place, own, sib, *weights, *acc)


def slot_kernel(p, place, *refs):
    write_slots(place, p, *refs)


def slots(place, p, dg, du, wg, wu):
    rows, hidden_count = dg.shape
    width = wg.shape[0] // 8
    return call(
        functools.partial(slot_kernel, p),
        (shape((rows, width), F32), shape((rows, width), BF16)),
        [SMEM] + [VMEM] * 4,
        [VMEM] * 2,
        8 * rows * width * hidden_count,
        0,
    )(place, dg, du, wg, wu)


def weight_kernel(jobs, begun, place, *refs):
    n = len(jobs)
    own, sib, ds = refs[0:4], refs[4:8], refs[8 : 8 + n]
    refs = refs[8 + n + begun :]
    outs, bufs, sems = refs[:n], refs[n : 2 * n], refs[2 * n]
    core = place[0] % 2
    wide = 2 * own[0].shape[2]
    chips = far(place)
    copies = []
    for i, ((array, pieces), d, out, buf) in enumerate(zip(jobs, ds, outs, bufs)):
        for j, p in enumerate(pieces):
            rows = block_at(place, chips[p], wide)
            piece = both_cores(core, own[p][array], sib[p][array])
            if array == 0:
                buf[j] = dot(piece, d[...], 0, 0).astype(BF16)
                target = out.at[rows, :]
            else:
                buf[j] = dot(d[...], piece, 0, 0).astype(BF16)
                target = out.at[:, rows]
            copies.append(pltpu.make_async_copy(buf.at[j], target, sems.at[i, j]))
            copies[-1].start()
    for copy in copies:
        copy.wait()


def weight_grads(place, jobs, own, sib, ds, begun=None):
    rows, width = own[0].shape[1:]
    hidden_count = ds[0].shape[1]
    blocks = [(2 * width, hidden_count) if array == 0 else (hidden_count, 2 * width) for array, _ in jobs]
    outs = [(8 * width, hidden_count) if array == 0 else (hidden_count, 8 * width) for array, _ in jobs]
    count = sum(len(pieces) for _, pieces in jobs)
    more = [] if begun is None else [begun]
    return call(
        functools.partial(weight_kernel, jobs, len(more)),
        tuple(shape(out, BF16) for out in outs),
        [SMEM] + [VMEM] * (8 + len(ds)) + [HBM] * len(more),
        [HBM] * len(ds),
        4 * rows * width * hidden_count * count,
        4 * width * hidden_count * count,
        scratch=[pltpu.VMEM((len(pieces),) + block, BF16) for block, (_, pieces) in zip(blocks, jobs)]
        + [pltpu.SemaphoreType.DMA((len(ds), 4))],
        limit=LOAD_LIMIT,
        aliases={9 + len(ds): 0} if more else {},
    )(place, *own, *sib, *ds, *more)


def pack_kernel(groups, place, *refs):
    sources, outs, here, sems = refs[:4], refs[4 : 4 + groups], refs[4 + groups : 8 + groups], refs[8 + groups]
    copies = [pltpu.make_async_copy(s, d, sems.at[i]) for i, (s, d) in enumerate(zip(sources, here))]
    for copy in copies:
        copy.start()
    for copy in copies:
        copy.wait()
    acts, grad, routing, gates = here
    wide = grad[...].astype(F32)
    for distance, out in enumerate(outs):
        expert = lax.rem(place[0] + distance, groups)
        gate = jnp.sum(jnp.where(routing[...] == expert, gates[...], 0.0), axis=0, keepdims=True)
        out[0] = acts[...]
        out[1] = (wide * gate.T).astype(BF16)


def pack(place, acts, grad, routing, gates, groups):
    sources = (acts, grad, routing.T, gates.T)
    return call(
        functools.partial(pack_kernel, groups),
        (shape((2,) + acts.shape, BF16),) * groups,
        [SMEM] + [HBM] * 4,
        [VMEM] * groups,
        1,
        1,
        scratch=[pltpu.VMEM(s.shape, s.dtype) for s in sources] + [pltpu.SemaphoreType.DMA((4,))],
        limit=63,
    )(place, *sources)


def across(array, even, odd=None):
    masks = (even, even if odd is None else odd)
    return lax.ppermute(array, "tensor", [(i, i ^ masks[i % 2]) for i in range(8)])


def along(array, distance, count):
    return lax.ppermute(array, "expert", [(i, (i + distance) % count) for i in range(count)])


def chips_body(acts, grad_out, routing, gates, w_gate, w_up, w_down):
    groups = lax.axis_size("expert")
    place = lax.axis_index("tensor").astype(jnp.int32)[None]
    z = lax.axis_index("expert").astype(jnp.int32)[None]
    tok_count, width = acts.shape
    packed = pack(z, acts, grad_out, routing, gates, groups)
    blocks = [packed[0]] + [along(packed[k], k, groups) for k in range(1, groups)]
    own = jnp.concatenate(blocks, axis=1)
    near = across(own, 1)
    here = across(own, 2, 4), across(near, 2, 4)
    wg, wu, gate, up = load(place, own, near, w_gate[0], w_up[0])
    first, gate, up = lax.optimization_barrier((here[0], gate, up))
    diag = across(first, 4, 2)
    there_second = across(first, 1)
    wd = w_down[0]
    back = own_back(place, own, near, wd)
    second, back = lax.optimization_barrier((here[1], back))
    there_first = across(second, 1)
    weights, acc = (wg, wu, wd), (gate, up, back)
    acc = partial_sums(place, 1, first, second, weights, acc)
    diag, acc = lax.optimization_barrier((diag, acc))
    diag_near = across(diag, 1)
    acc = partial_sums(place, 2, there_first, there_second, weights, acc)
    hid, dg, du, keep, send = middle(place, diag, diag_near, weights, acc)
    mine_of = own, first, there_first, diag
    other_of = near, second, there_second, diag_near

    def chip_sum(keep, send):
        return keep + across(send, 1).astype(F32)

    shares = {1: slots(place, 1, dg, du, wg, wu)}
    total, dg, du = lax.optimization_barrier((chip_sum(keep, send), dg, du))
    parts = [across(total.astype(BF16), 6)]
    shares[2] = slots(place, 2, dg, du, wg, wu)
    parts.append(across(chip_sum(*shares[1]).astype(BF16), 2))
    total, dg, du = lax.optimization_barrier((chip_sum(*shares[2]), dg, du))
    parts.append(across(total.astype(BF16), 4))
    share = slots(place, 0, dg, du, wg, wu)
    share, dg = lax.optimization_barrier((share, dg))
    (grad_gate,) = weight_grads(place, [(0, (0, 1))], mine_of, other_of, (dg,))
    mine = chip_sum(*share)
    parts[0], dg, grad_gate = lax.optimization_barrier((parts[0], dg, grad_gate))
    grad_gate, grad_up = weight_grads(
        place, [(0, (2, 3)), (0, UP_FIRST)], mine_of, other_of, (dg, du), grad_gate
    )
    for part in parts:
        mine = mine + part.astype(F32)
    mine, hid, grad_up = lax.optimization_barrier((mine, hid, grad_up))
    grad_up, grad_down = weight_grads(
        place, [(0, UP_LAST), (1, (0, 1, 2, 3))], mine_of, other_of, (du, hid), grad_up
    )
    mine = mine.reshape(groups, tok_count, width)
    back = mine[0]
    sent = mine.astype(BF16)
    for k in range(1, groups):
        back = back + along(sent[k], -k, groups).astype(F32)
    return (grad_gate[None], grad_up[None], grad_down[None], back.astype(BF16))


def any_body(acts, grad_out, routing, gates, w_gate, w_up, w_down):
    expert = lax.axis_index("expert")
    acts_all, grad_all = (
        lax.all_gather(
            lax.all_gather(array, "tensor", axis=1, tiled=True), "expert", axis=0, tiled=True
        )
        for array in (acts, grad_out)
    )
    routing_all = lax.all_gather(routing, "expert", axis=0, tiled=True)
    gates_all = lax.all_gather(gates, "expert", axis=0, tiled=True)
    grad_all = (grad_all.astype(F32) * gate_of(routing_all, gates_all, expert)).astype(BF16)
    wg, wu, wd = w_gate[0], w_up[0], w_down[0]
    hid, dg, du = hidden_grads(dot(acts_all, wg, 1, 0), dot(acts_all, wu, 1, 0), dot(grad_all, wd, 1, 1))
    partial = dot(dg, wg, 1, 1) + dot(du, wu, 1, 1)
    partial = lax.psum_scatter(partial, "tensor", scatter_dimension=1, tiled=True)
    back = lax.psum_scatter(partial, "expert", scatter_dimension=0, tiled=True)
    return (
        dot(acts_all, dg, 0, 0).astype(BF16)[None],
        dot(acts_all, du, 0, 0).astype(BF16)[None],
        dot(hid, grad_all, 0, 0).astype(BF16)[None],
        back.astype(BF16),
    )


def solution(mesh):
    chips = mesh.shape["tensor"] == 8
    return jax.shard_map(
        chips_body if chips else any_body,
        mesh=mesh,
        in_specs=(
            P("expert", "tensor"),
            P("expert", "tensor"),
            P("expert", None),
            P("expert", None),
            P("expert", None, "tensor"),
            P("expert", None, "tensor"),
            P("expert", "tensor", None),
        ),
        out_specs=(
            P("expert", None, "tensor"),
            P("expert", None, "tensor"),
            P("expert", "tensor", None),
            P("expert", "tensor"),
        ),
        check_vma=False,
    )
```

```python
import functools

import jax
import jax.numpy as jnp
from jax import lax
from jax.experimental import pallas as pl
from jax.experimental.pallas import tpu as pltpu
from jax.sharding import PartitionSpec as P

F32 = jnp.float32
BF16 = jnp.bfloat16


def dot(left, right, left_dim, right_dim):
    return lax.dot_general(
        left, right, (((left_dim,), (right_dim,)), ((), ())), preferred_element_type=F32
    )


def gate_of(routing, gates, expert):
    return jnp.sum(jnp.where(routing == expert, gates, 0.0), axis=1, keepdims=True)


def hidden_grads(gate_pre, up_pre, grad_hidden):
    sig = jax.nn.sigmoid(gate_pre)
    act = gate_pre * sig
    hidden = (act * up_pre).astype(BF16)
    grad_up_pre = (grad_hidden * act).astype(BF16)
    grad_gate_pre = (grad_hidden * up_pre * sig * (1.0 + gate_pre * (1.0 - sig))).astype(BF16)
    return hidden, grad_gate_pre, grad_up_pre


VMEM = pl.BlockSpec(memory_space=pltpu.VMEM)
SMEM = pl.BlockSpec(memory_space=pltpu.SMEM)
HBM = pl.BlockSpec(memory_space=pl.ANY)


def shape(dims, dtype):
    return jax.ShapeDtypeStruct(dims, dtype)


def call(kernel, out_shape, in_specs, out_specs, flops, moved, scratch=(), limit=16, aliases={}):
    return pl.pallas_call(
        kernel,
        out_shape=out_shape,
        in_specs=in_specs,
        out_specs=out_specs,
        scratch_shapes=scratch,
        input_output_aliases=aliases,
        compiler_params=pltpu.CompilerParams(vmem_limit_bytes=limit * 1024 * 1024),
        cost_estimate=pl.CostEstimate(flops=flops, bytes_accessed=moved, transcendentals=0),
    )


def both_cores(core, mine, other):
    first = core == 0
    return jnp.concatenate([jnp.where(first, mine, other), jnp.where(first, other, mine)], axis=1)


def block_at(place, p, wide):
    return pl.ds(pl.multiple_of((place[0] // 2 ^ p) * wide, wide), wide)


STEP = 256
LOAD_LIMIT = 28
PARTS = 2


def far(place):
    core = place[0] % 2
    return 0, 1 + core, 2 - core, 3


def pair(place, i, own, sib):
    core = place[0] % 2
    rows = block_at(place, far(place)[i], 2 * own.shape[2])
    return rows, both_cores(core, own[0], sib[0]), both_cores(core, own[1], sib[1])


def add_pieces(pieces, weights, acc_in, acc_out, finish):
    wg, wu, wd = weights
    for f in range(wg.shape[1] // STEP):
        cols = pl.ds(f * STEP, STEP)
        sums = [None if acc is None else acc[:, cols] for acc in acc_in]
        for rows, x, g in pieces:
            terms = (dot(x, wg[rows, cols], 1, 0), dot(x, wu[rows, cols], 1, 0), dot(g, wd[cols, rows], 1, 1))
            sums = [t if s is None else s + t for s, t in zip(sums, terms)]
        finish(cols, sums, acc_out)


def store(cols, sums, outs):
    for out, value in zip(outs, sums):
        out[:, cols] = value


def store_grads(cols, sums, outs):
    store(cols, hidden_grads(*sums), outs)


def turn(block, out):
    for c in range(0, block.shape[1], STEP):
        out[c : c + STEP, :] = block[:, c : c + STEP].T


def load_kernel(place, own, near, *refs):
    sources, here, sums, sems = refs[:2], refs[2:4], refs[4:6], refs[6]
    row, x, _ = pair(place, 0, own, near)
    wide = x.shape[1]
    copies = []
    for p in range(4):
        rows = block_at(place, p, wide)
        for i, (s, h) in enumerate(zip(sources, here)):
            copies.append(pltpu.make_async_copy(s.at[rows, :], h.at[rows, :], sems.at[i, p]))
            copies[-1].start()
    for copy, weight, total in zip(copies, here, sums):
        copy.wait()
        for f in range(weight.shape[1] // STEP):
            cols = pl.ds(f * STEP, STEP)
            total[:, cols] = dot(x, weight[row, cols], 1, 0)
    for copy in copies[2:]:
        copy.wait()


def load(place, own, near, wg, wu):
    rows, hidden_count = own.shape[1], wg.shape[1]
    return call(
        load_kernel,
        (shape(wg.shape, BF16),) * 2 + (shape((rows, hidden_count), F32),) * 2,
        [SMEM] + [VMEM] * 2 + [HBM] * 2,
        [VMEM] * 4,
        1,
        1,
        scratch=[pltpu.SemaphoreType.DMA((2, 4))],
        limit=36,
    )(place, own, near, wg, wu)


def back_kernel(place, own, near, wd, back):
    row, _, g = pair(place, 0, own, near)
    for f in range(wd.shape[0] // STEP):
        cols = pl.ds(f * STEP, STEP)
        back[:, cols] = dot(g, wd[cols, row], 1, 1)


def own_back(place, own, near, wd):
    rows, hidden_count = own.shape[1], wd.shape[0]
    return call(
        back_kernel, shape((rows, hidden_count), F32), [SMEM] + [VMEM] * 3, VMEM, 1, 1
    )(place, own, near, wd)


def partial_kernel(i, place, own, sib, wg, wu, wd, *refs):
    add_pieces([pair(place, i, own, sib)], (wg, wu, wd), refs[:3], refs[3:6], store)
    for weight, out in zip((wu,), refs[6:]):
        for p in range(4):
            turn(weight[block_at(place, p, out.shape[2]), :], out.at[p])


def partial_sums(place, i, own, sib, weights, acc, turned=False):
    rows, hidden_count = acc[0].shape
    more = (shape((4, hidden_count, weights[1].shape[0] // 4), BF16),) * 1 if turned else ()
    return call(
        functools.partial(partial_kernel, i),
        (shape((rows, hidden_count), F32),) * 3 + more,
        [SMEM] + [VMEM] * 8,
        [VMEM] * (3 + len(more)),
        1,
        1,
        aliases={6: 0, 7: 1, 8: 2},
    )(place, own, sib, *weights, *acc)


def write_slots(place, p, dg, du, wg, wu, keep, send):
    width = keep.shape[1]
    first = place[0] % 2 == 0
    part = dot(dg[...], wg[block_at(place, p, 2 * width), :], 1, 1) + dot(du[...], wu[p], 1, 0)
    low, high = part[:, :width], part[:, width:]
    keep[...] = jnp.where(first, low, high)
    send[...] = jnp.where(first, high, low).astype(BF16)


def middle_kernel(place, own, sib, wg, wu, wd, gate, up, back, hid, dg, du, keep, send):
    rows, x, g = pair(place, 3, own, sib)
    for f in range(wd.shape[0] // STEP):
        cols = pl.ds(f * STEP, STEP)
        sums = (
            gate[:, cols] + dot(x, wg[rows, cols], 1, 0),
            up[:, cols] + dot(x, wu[3, cols, :], 1, 1),
            back[:, cols] + dot(g, wd[cols, rows], 1, 1),
        )
        store_grads(cols, sums, (hid, dg, du))
    write_slots(place, 3, dg, du, wg, wu, keep, send)


def middle(place, own, sib, turned, wd, acc):
    rows, width = own.shape[1:]
    hidden_count = wd.shape[0]
    return call(
        middle_kernel,
        (shape((rows, hidden_count), BF16),) * 3 + (shape((rows, width), F32), shape((rows, width), BF16)),
        [SMEM] + [VMEM] * 8,
        [VMEM] * 5,
        20 * rows * width * hidden_count,
        0,
    )(place, own, sib, *turned, wd, *acc)


def slot_kernel(p, place, *refs):
    write_slots(place, p, *refs)


def slots(place, p, dg, du, turned):
    rows, hidden_count = dg.shape
    width = turned[1].shape[2] // 2
    return call(
        functools.partial(slot_kernel, p),
        (shape((rows, width), F32), shape((rows, width), BF16)),
        [SMEM] + [VMEM] * 4,
        [VMEM] * 2,
        8 * rows * width * hidden_count,
        0,
    )(place, dg, du, *turned)


def weight_kernel(jobs, begun, place, *refs):
    n = len(jobs)
    own, sib, ds = refs[0:4], refs[4:8], refs[8 : 8 + n]
    refs = refs[8 + n + begun :]
    outs, bufs, sems = refs[:n], refs[n : 2 * n], refs[2 * n]
    core = place[0] % 2
    wide = 2 * own[0].shape[2]
    chips = far(place)
    copies = []
    for i, ((array, pieces), d, out, buf) in enumerate(zip(jobs, ds, outs, bufs)):
        for j, p in enumerate(pieces):
            rows = block_at(place, chips[p], wide)
            piece = both_cores(core, own[p][array], sib[p][array])
            left, right = (piece, d[...]) if array == 0 else (d[...], piece)
            size = left.shape[1] // PARTS
            for k in range(PARTS):
                part = pl.ds(k * size, size)
                buf[j, part, :] = dot(left[:, k * size : (k + 1) * size], right, 0, 0).astype(BF16)
                if array == 0:
                    start = pl.multiple_of((place[0] // 2 ^ chips[p]) * wide + k * size, size)
                    target = out.at[pl.ds(start, size), :]
                else:
                    target = out.at[part, rows]
                copies.append(pltpu.make_async_copy(buf.at[j, part, :], target, sems.at[i, j, k]))
                copies[-1].start()
    for copy in copies:
        copy.wait()


def weight_grads(place, jobs, own, sib, ds, begun=None):
    rows, width = own[0].shape[1:]
    hidden_count = ds[0].shape[1]
    blocks = [(2 * width, hidden_count) if array == 0 else (hidden_count, 2 * width) for array, _ in jobs]
    outs = [(8 * width, hidden_count) if array == 0 else (hidden_count, 8 * width) for array, _ in jobs]
    count = sum(len(pieces) for _, pieces in jobs)
    more = [] if begun is None else [begun]
    return call(
        functools.partial(weight_kernel, jobs, len(more)),
        tuple(shape(out, BF16) for out in outs),
        [SMEM] + [VMEM] * (8 + len(ds)) + [HBM] * len(more),
        [HBM] * len(ds),
        4 * rows * width * hidden_count * count,
        4 * width * hidden_count * count,
        scratch=[pltpu.VMEM((len(pieces),) + block, BF16) for block, (_, pieces) in zip(blocks, jobs)]
        + [pltpu.SemaphoreType.DMA((len(ds), 4, PARTS))],
        limit=LOAD_LIMIT,
        aliases={9 + len(ds): 0} if more else {},
    )(place, *own, *sib, *ds, *more)


def pack_kernel(groups, place, *refs):
    sources, outs, here, sems = refs[:4], refs[4 : 4 + groups], refs[4 + groups : 8 + groups], refs[8 + groups]
    copies = [pltpu.make_async_copy(s, d, sems.at[i]) for i, (s, d) in enumerate(zip(sources, here))]
    for copy in copies:
        copy.start()
    for copy in copies:
        copy.wait()
    acts, grad, routing, gates = here
    wide = grad[...].astype(F32)
    for distance, out in enumerate(outs):
        expert = lax.rem(place[0] + distance, groups)
        gate = jnp.sum(jnp.where(routing[...] == expert, gates[...], 0.0), axis=0, keepdims=True)
        out[0] = acts[...]
        out[1] = (wide * gate.T).astype(BF16)


def pack(place, acts, grad, routing, gates, groups):
    sources = (acts, grad, routing.T, gates.T)
    return call(
        functools.partial(pack_kernel, groups),
        (shape((2,) + acts.shape, BF16),) * groups,
        [SMEM] + [HBM] * 4,
        [VMEM] * groups,
        1,
        1,
        scratch=[pltpu.VMEM(s.shape, s.dtype) for s in sources] + [pltpu.SemaphoreType.DMA((4,))],
        limit=63,
    )(place, *sources)


def across(array, even, odd=None):
    masks = (even, even if odd is None else odd)
    return lax.ppermute(array, "tensor", [(i, i ^ masks[i % 2]) for i in range(8)])


def along(array, distance, count):
    return lax.ppermute(array, "expert", [(i, (i + distance) % count) for i in range(count)])


def chips_body(acts, grad_out, routing, gates, w_gate, w_up, w_down):
    groups = lax.axis_size("expert")
    place = lax.axis_index("tensor").astype(jnp.int32)[None]
    z = lax.axis_index("expert").astype(jnp.int32)[None]
    tok_count, width = acts.shape
    packed = pack(z, acts, grad_out, routing, gates, groups)
    blocks = [packed[0]] + [along(packed[k], k, groups) for k in range(1, groups)]
    own = jnp.concatenate(blocks, axis=1)
    near = across(own, 1)
    here = across(own, 2, 4), across(near, 2, 4)
    wg, wu, gate, up = load(place, own, near, w_gate[0], w_up[0])
    first, gate, up = lax.optimization_barrier((here[0], gate, up))
    diag = across(first, 4, 2)
    there_second = across(first, 1)
    wd = w_down[0]
    back = own_back(place, own, near, wd)
    second, back = lax.optimization_barrier((here[1], back))
    there_first = across(second, 1)
    weights, acc = (wg, wu, wd), (gate, up, back)
    *acc, wu_turned = partial_sums(place, 1, first, second, weights, acc, True)
    turned = wg, wu_turned
    diag, acc = lax.optimization_barrier((diag, acc))
    diag_near = across(diag, 1)
    acc = partial_sums(place, 2, there_first, there_second, weights, acc)
    hid, dg, du, keep, send = middle(place, diag, diag_near, turned, wd, acc)
    mine_of = own, first, there_first, diag
    other_of = near, second, there_second, diag_near

    def chip_sum(keep, send):
        return keep + across(send, 1).astype(F32)

    shares = {1: slots(place, 1, dg, du, turned)}
    total, dg, du = lax.optimization_barrier((chip_sum(keep, send), dg, du))
    parts = [across(total.astype(BF16), 6)]
    shares[2] = slots(place, 2, dg, du, turned)
    parts.append(across(chip_sum(*shares[1]).astype(BF16), 2))
    total, dg, du = lax.optimization_barrier((chip_sum(*shares[2]), dg, du))
    parts.append(across(total.astype(BF16), 4))
    share = slots(place, 0, dg, du, turned)
    share, dg = lax.optimization_barrier((share, dg))
    (grad_gate,) = weight_grads(place, [(0, (0, 1))], mine_of, other_of, (dg,))
    mine = chip_sum(*share)
    parts[0], dg, grad_gate = lax.optimization_barrier((parts[0], dg, grad_gate))
    (grad_gate,) = weight_grads(place, [(0, (2, 3))], mine_of, other_of, (dg,), grad_gate)
    for part in parts:
        mine = mine + part.astype(F32)
    mine, hid, grad_gate = lax.optimization_barrier((mine, hid, grad_gate))
    whole = (0, 1, 2, 3)
    grad_up, grad_down = weight_grads(place, [(0, whole), (1, whole)], mine_of, other_of, (du, hid))
    mine = mine.reshape(groups, tok_count, width)
    back = mine[0]
    sent = mine.astype(BF16)
    for k in range(1, groups):
        back = back + along(sent[k], -k, groups).astype(F32)
    return (grad_gate[None], grad_up[None], grad_down[None], back.astype(BF16))


def any_body(acts, grad_out, routing, gates, w_gate, w_up, w_down):
    expert = lax.axis_index("expert")
    acts_all, grad_all = (
        lax.all_gather(
            lax.all_gather(array, "tensor", axis=1, tiled=True), "expert", axis=0, tiled=True
        )
        for array in (acts, grad_out)
    )
    routing_all = lax.all_gather(routing, "expert", axis=0, tiled=True)
    gates_all = lax.all_gather(gates, "expert", axis=0, tiled=True)
    grad_all = (grad_all.astype(F32) * gate_of(routing_all, gates_all, expert)).astype(BF16)
    wg, wu, wd = w_gate[0], w_up[0], w_down[0]
    hid, dg, du = hidden_grads(dot(acts_all, wg, 1, 0), dot(acts_all, wu, 1, 0), dot(grad_all, wd, 1, 1))
    partial = dot(dg, wg, 1, 1) + dot(du, wu, 1, 1)
    partial = lax.psum_scatter(partial, "tensor", scatter_dimension=1, tiled=True)
    back = lax.psum_scatter(partial, "expert", scatter_dimension=0, tiled=True)
    return (
        dot(acts_all, dg, 0, 0).astype(BF16)[None],
        dot(acts_all, du, 0, 0).astype(BF16)[None],
        dot(hid, grad_all, 0, 0).astype(BF16)[None],
        back.astype(BF16),
    )


def solution(mesh):
    chips = mesh.shape["tensor"] == 8
    return jax.shard_map(
        chips_body if chips else any_body,
        mesh=mesh,
        in_specs=(
            P("expert", "tensor"),
            P("expert", "tensor"),
            P("expert", None),
            P("expert", None),
            P("expert", None, "tensor"),
            P("expert", None, "tensor"),
            P("expert", "tensor", None),
        ),
        out_specs=(
            P("expert", None, "tensor"),
            P("expert", None, "tensor"),
            P("expert", "tensor", None),
            P("expert", "tensor"),
        ),
        check_vma=False,
    )
```

```python
import functools

import jax
import jax.numpy as jnp
from jax import lax
from jax.experimental import pallas as pl
from jax.experimental.pallas import tpu as pltpu
from jax.sharding import PartitionSpec as P

F32 = jnp.float32
BF16 = jnp.bfloat16


def dot(left, right, left_dim, right_dim):
    return lax.dot_general(
        left, right, (((left_dim,), (right_dim,)), ((), ())), preferred_element_type=F32
    )


def gate_of(routing, gates, expert):
    return jnp.sum(jnp.where(routing == expert, gates, 0.0), axis=1, keepdims=True)


def hidden_grads(gate_pre, up_pre, grad_hidden):
    sig = jax.nn.sigmoid(gate_pre)
    act = gate_pre * sig
    hidden = (act * up_pre).astype(BF16)
    grad_up_pre = (grad_hidden * act).astype(BF16)
    grad_gate_pre = (grad_hidden * up_pre * sig * (1.0 + gate_pre * (1.0 - sig))).astype(BF16)
    return hidden, grad_gate_pre, grad_up_pre


VMEM = pl.BlockSpec(memory_space=pltpu.VMEM)
SMEM = pl.BlockSpec(memory_space=pltpu.SMEM)
HBM = pl.BlockSpec(memory_space=pl.ANY)


def in_hbm(array):
    return pltpu.with_memory_space_constraint(array, pltpu.HBM)


def shape(dims, dtype):
    return jax.ShapeDtypeStruct(dims, dtype)


def call(kernel, out_shape, in_specs, out_specs, flops, moved, scratch=(), limit=8, aliases={}):
    return pl.pallas_call(
        kernel,
        out_shape=out_shape,
        in_specs=in_specs,
        out_specs=out_specs,
        scratch_shapes=scratch,
        input_output_aliases=aliases,
        compiler_params=pltpu.CompilerParams(vmem_limit_bytes=limit * 1024 * 1024),
        cost_estimate=pl.CostEstimate(flops=flops, bytes_accessed=moved, transcendentals=0),
    )


def both_cores(core, mine, other):
    first = core == 0
    return jnp.concatenate([jnp.where(first, mine, other), jnp.where(first, other, mine)], axis=1)


def block_at(place, p, wide):
    return pl.ds(pl.multiple_of((place[0] // 2 ^ p) * wide, wide), wide)


STEP = 256
LOAD_LIMIT = 28
PARTS = 2


def far(place):
    core = place[0] % 2
    return 0, 1 + core, 2 - core, 3


def pair(place, i, own, sib):
    core = place[0] % 2
    rows = block_at(place, far(place)[i], 2 * own.shape[2])
    return rows, both_cores(core, own[0], sib[0]), both_cores(core, own[1], sib[1])


def add_pieces(pieces, weights, acc_in, acc_out, finish):
    wg, wu, wd = weights
    for f in range(wg.shape[1] // STEP):
        cols = pl.ds(f * STEP, STEP)
        sums = [None if acc is None else acc[:, cols] for acc in acc_in]
        for rows, x, g in pieces:
            terms = (dot(x, wg[rows, cols], 1, 0), dot(x, wu[rows, cols], 1, 0), dot(g, wd[cols, rows], 1, 1))
            sums = [t if s is None else s + t for s, t in zip(sums, terms)]
        finish(cols, sums, acc_out)


def store(cols, sums, outs):
    for out, value in zip(outs, sums):
        out[:, cols] = value


def store_grads(cols, sums, outs):
    store(cols, hidden_grads(*sums), outs)


def turn(block, out):
    for c in range(0, block.shape[1], STEP):
        out[c : c + STEP, :] = block[:, c : c + STEP].T


def load_kernel(place, own, near, *refs):
    sources, here, sums, turned, sems = refs[:2], refs[2:4], refs[4:6], refs[6], refs[7]
    row, x, _ = pair(place, 0, own, near)
    wide = x.shape[1]
    copies = []
    for p in range(4):
        rows = block_at(place, p, wide)
        for i, (s, h) in enumerate(zip(sources, here)):
            copies.append(pltpu.make_async_copy(s.at[rows, :], h.at[rows, :], sems.at[i, p]))
            copies[-1].start()
    for copy, weight, total in zip(copies, here, sums):
        copy.wait()
        for f in range(weight.shape[1] // STEP):
            cols = pl.ds(f * STEP, STEP)
            total[:, cols] = dot(x, weight[row, cols], 1, 0)
    for p in range(4):
        if p > 0:
            copies[2 * p].wait()
        turn(here[0][block_at(place, p, wide), :], turned.at[p])
    for copy in copies[3::2]:
        copy.wait()


def load(place, own, near, wg, wu):
    rows, hidden_count = own.shape[1], wg.shape[1]
    return call(
        load_kernel,
        (shape(wg.shape, BF16),) * 2
        + (shape((rows, hidden_count), F32),) * 2
        + (shape((4, hidden_count, wg.shape[0] // 4), BF16),),
        [SMEM] + [VMEM] * 2 + [HBM] * 2,
        [VMEM] * 5,
        1,
        1,
        scratch=[pltpu.SemaphoreType.DMA((2, 4))],
        limit=16,
    )(place, own, near, in_hbm(wg), in_hbm(wu))


def back_kernel(place, own, near, wd, back):
    row, _, g = pair(place, 0, own, near)
    for f in range(wd.shape[0] // STEP):
        cols = pl.ds(f * STEP, STEP)
        back[:, cols] = dot(g, wd[cols, row], 1, 1)


def own_back(place, own, near, wd):
    rows, hidden_count = own.shape[1], wd.shape[0]
    return call(
        back_kernel, shape((rows, hidden_count), F32), [SMEM] + [VMEM] * 3, VMEM, 1, 1
    )(place, own, near, wd)


def partial_kernel(place, own, sib, wg, wu, wd, *refs):
    add_pieces([pair(place, 1, own, sib)], (wg, wu, wd), refs[:3], refs[3:6], store)
    up_turned, down_turned = refs[6:]
    wide = up_turned.shape[2]
    for i in range(2):
        rows = block_at(place, far(place)[2 + i], wide)
        for f in range(0, wd.shape[0], STEP):
            down_turned[i, :, f : f + STEP] = wd[f : f + STEP, rows].T
    for p in range(4):
        turn(wu[block_at(place, p, wide), :], up_turned.at[p])


def partial_sums(place, own, sib, weights, acc):
    rows, hidden_count = acc[0].shape
    wide = weights[1].shape[0] // 4
    return call(
        partial_kernel,
        (shape((rows, hidden_count), F32),) * 3
        + (shape((4, hidden_count, wide), BF16), shape((2, wide, hidden_count), BF16)),
        [SMEM] + [VMEM] * 8,
        [VMEM] * 5,
        1,
        1,
        aliases={6: 0, 7: 1, 8: 2},
    )(place, own, sib, *weights, *acc)


def third_kernel(place, own, sib, wg, wu, wd, gate_in, up_in, back_in, gate, up, back):
    rows, x, g = pair(place, 2, own, sib)
    for f in range(wg.shape[1] // STEP):
        cols = pl.ds(f * STEP, STEP)
        gate[:, cols] = gate_in[:, cols] + dot(x, wg[rows, cols], 1, 0)
        up[:, cols] = up_in[:, cols] + dot(x, wu[rows, cols], 1, 0)
        back[:, cols] = back_in[:, cols] + dot(g, wd[0, :, cols], 1, 0)


def third_sums(place, own, sib, weights, acc):
    return call(
        third_kernel,
        (shape(acc[0].shape, F32),) * 3,
        [SMEM] + [VMEM] * 8,
        [VMEM] * 3,
        1,
        1,
        aliases={6: 0, 7: 1, 8: 2},
    )(place, own, sib, *weights, *acc)


def write_slots(place, p, dg, du, wg, wu, keep, send):
    width = keep.shape[1]
    first = place[0] % 2 == 0
    part = dot(dg[...], wg[p], 1, 0) + dot(du[...], wu[p], 1, 0)
    low, high = part[:, :width], part[:, width:]
    keep[...] = jnp.where(first, low, high)
    send[...] = jnp.where(first, high, low).astype(BF16)


def middle_kernel(place, own, sib, wg, wu, wd, gate, up, back, hid, dg, du, keep, send):
    rows, x, g = pair(place, 3, own, sib)
    for f in range(wd.shape[2] // STEP):
        cols = pl.ds(f * STEP, STEP)
        sums = (
            gate[:, cols] + dot(x, wg[3, cols, :], 1, 1),
            up[:, cols] + dot(x, wu[3, cols, :], 1, 1),
            back[:, cols] + dot(g, wd[1, :, cols], 1, 0),
        )
        store_grads(cols, sums, (hid, dg, du))
    write_slots(place, 3, dg, du, wg, wu, keep, send)


def middle(place, own, sib, turned, wd, acc):
    rows, width = own.shape[1:]
    hidden_count = wd.shape[2]
    return call(
        middle_kernel,
        (shape((rows, hidden_count), BF16),) * 3 + (shape((rows, width), F32), shape((rows, width), BF16)),
        [SMEM] + [VMEM] * 8,
        [VMEM] * 5,
        20 * rows * width * hidden_count,
        0,
    )(place, own, sib, *turned, wd, *acc)


def slot_kernel(p, place, *refs):
    write_slots(place, p, *refs)


def slots(place, p, dg, du, turned):
    rows, hidden_count = dg.shape
    width = turned[1].shape[2] // 2
    return call(
        functools.partial(slot_kernel, p),
        (shape((rows, width), F32), shape((rows, width), BF16)),
        [SMEM] + [VMEM] * 4,
        [VMEM] * 2,
        8 * rows * width * hidden_count,
        0,
    )(place, dg, du, *turned)


def weight_kernel(jobs, begun, place, *refs):
    n = len(jobs)
    own, sib, ds = refs[0:4], refs[4:8], refs[8 : 8 + n]
    refs = refs[8 + n + begun :]
    outs, bufs, sems = refs[:n], refs[n : 2 * n], refs[2 * n]
    core = place[0] % 2
    wide = 2 * own[0].shape[2]
    chips = far(place)
    copies = []
    for i, ((array, pieces), d, out, buf) in enumerate(zip(jobs, ds, outs, bufs)):
        for j, p in enumerate(pieces):
            rows = block_at(place, chips[p], wide)
            piece = both_cores(core, own[p][array], sib[p][array])
            left, right = (piece, d[...]) if array == 0 else (d[...], piece)
            size = left.shape[1] // PARTS
            for k in range(PARTS):
                part = pl.ds(k * size, size)
                buf[j, part, :] = dot(left[:, k * size : (k + 1) * size], right, 0, 0).astype(BF16)
                if array == 0:
                    start = pl.multiple_of((place[0] // 2 ^ chips[p]) * wide + k * size, size)
                    target = out.at[pl.ds(start, size), :]
                else:
                    target = out.at[part, rows]
                copies.append(pltpu.make_async_copy(buf.at[j, part, :], target, sems.at[i, j, k]))
                copies[-1].start()
    for copy in copies:
        copy.wait()


def weight_grads(place, jobs, own, sib, ds, begun=None):
    rows, width = own[0].shape[1:]
    hidden_count = ds[0].shape[1]
    blocks = [(2 * width, hidden_count) if array == 0 else (hidden_count, 2 * width) for array, _ in jobs]
    outs = [(8 * width, hidden_count) if array == 0 else (hidden_count, 8 * width) for array, _ in jobs]
    count = sum(len(pieces) for _, pieces in jobs)
    more = [] if begun is None else [begun]
    return call(
        functools.partial(weight_kernel, jobs, len(more)),
        tuple(shape(out, BF16) for out in outs),
        [SMEM] + [VMEM] * (8 + len(ds)) + [HBM] * len(more),
        [HBM] * len(ds),
        4 * rows * width * hidden_count * count,
        4 * width * hidden_count * count,
        scratch=[pltpu.VMEM((len(pieces),) + block, BF16) for block, (_, pieces) in zip(blocks, jobs)]
        + [pltpu.SemaphoreType.DMA((len(ds), 4, PARTS))],
        limit=LOAD_LIMIT,
        aliases={9 + len(ds): 0} if more else {},
    )(place, *own, *sib, *ds, *more)


def pack_kernel(groups, place, *refs):
    sources, outs, here, sems = refs[:4], refs[4 : 4 + groups], refs[4 + groups : 8 + groups], refs[8 + groups]
    copies = [pltpu.make_async_copy(s, d, sems.at[i]) for i, (s, d) in enumerate(zip(sources, here))]
    for copy in copies:
        copy.start()
    for copy in copies:
        copy.wait()
    acts, grad, routing, gates = here
    wide = grad[...].astype(F32)
    for distance, out in enumerate(outs):
        expert = lax.rem(place[0] + distance, groups)
        gate = jnp.sum(jnp.where(routing[...] == expert, gates[...], 0.0), axis=0, keepdims=True)
        out[0] = acts[...]
        out[1] = (wide * gate.T).astype(BF16)


def pack(place, acts, grad, routing, gates, groups):
    sources = tuple(in_hbm(s) for s in (acts, grad, routing.T, gates.T))
    return call(
        functools.partial(pack_kernel, groups),
        (shape((2,) + acts.shape, BF16),) * groups,
        [SMEM] + [HBM] * 4,
        [VMEM] * groups,
        1,
        1,
        scratch=[pltpu.VMEM(s.shape, s.dtype) for s in sources] + [pltpu.SemaphoreType.DMA((4,))],
        limit=16,
    )(place, *sources)


def across(array, even, odd=None):
    masks = (even, even if odd is None else odd)
    return lax.ppermute(array, "tensor", [(i, i ^ masks[i % 2]) for i in range(8)])


def along(array, distance, count):
    return lax.ppermute(array, "expert", [(i, (i + distance) % count) for i in range(count)])


def chips_body(acts, grad_out, routing, gates, w_gate, w_up, w_down):
    groups = lax.axis_size("expert")
    place = lax.axis_index("tensor").astype(jnp.int32)[None]
    z = lax.axis_index("expert").astype(jnp.int32)[None]
    tok_count, width = acts.shape
    packed = pack(z, acts, grad_out, routing, gates, groups)
    blocks = [packed[0]] + [along(packed[k], k, groups) for k in range(1, groups)]
    own = jnp.concatenate(blocks, axis=1)
    near = across(own, 1)
    here = across(own, 2, 4), across(near, 2, 4)
    wg, wu, gate, up, wg_turned = load(place, own, near, w_gate[0], w_up[0])
    first, gate, up = lax.optimization_barrier((here[0], gate, up))
    diag = across(first, 4, 2)
    there_second = across(first, 1)
    wd = w_down[0]
    back = own_back(place, own, near, wd)
    second, back = lax.optimization_barrier((here[1], back))
    there_first = across(second, 1)
    weights, acc = (wg, wu, wd), (gate, up, back)
    *acc, wu_turned, wd_turned = partial_sums(place, first, second, weights, acc)
    turned = wg_turned, wu_turned
    diag, acc = lax.optimization_barrier((diag, acc))
    diag_near = across(diag, 1)
    acc = third_sums(place, there_first, there_second, (wg, wu, wd_turned), acc)
    hid, dg, du, keep, send = middle(place, diag, diag_near, turned, wd_turned, acc)
    mine_of = own, first, there_first, diag
    other_of = near, second, there_second, diag_near

    def chip_sum(keep, send):
        return keep + across(send, 1).astype(F32)

    shares = {1: slots(place, 1, dg, du, turned)}
    total, dg, du = lax.optimization_barrier((chip_sum(keep, send), dg, du))
    parts = [across(total.astype(BF16), 6)]
    shares[2] = slots(place, 2, dg, du, turned)
    parts.append(across(chip_sum(*shares[1]).astype(BF16), 2))
    total, dg, du = lax.optimization_barrier((chip_sum(*shares[2]), dg, du))
    parts.append(across(total.astype(BF16), 4))
    share = slots(place, 0, dg, du, turned)
    share, dg = lax.optimization_barrier((share, dg))
    (grad_gate,) = weight_grads(place, [(0, (0, 1))], mine_of, other_of, (dg,))
    mine = chip_sum(*share)
    parts[0], dg, grad_gate = lax.optimization_barrier((parts[0], dg, grad_gate))
    (grad_gate,) = weight_grads(place, [(0, (2, 3))], mine_of, other_of, (dg,), grad_gate)
    for part in parts:
        mine = mine + part.astype(F32)
    mine, hid, grad_gate = lax.optimization_barrier((mine, hid, grad_gate))
    whole = (0, 1, 2, 3)
    grad_up, grad_down = weight_grads(place, [(0, whole), (1, whole)], mine_of, other_of, (du, hid))
    mine = mine.reshape(groups, tok_count, width)
    back = mine[0]
    sent = mine.astype(BF16)
    for k in range(1, groups):
        back = back + along(sent[k], -k, groups).astype(F32)
    return (grad_gate[None], grad_up[None], grad_down[None], back.astype(BF16))


def any_body(acts, grad_out, routing, gates, w_gate, w_up, w_down):
    expert = lax.axis_index("expert")
    acts_all, grad_all = (
        lax.all_gather(
            lax.all_gather(array, "tensor", axis=1, tiled=True), "expert", axis=0, tiled=True
        )
        for array in (acts, grad_out)
    )
    routing_all = lax.all_gather(routing, "expert", axis=0, tiled=True)
    gates_all = lax.all_gather(gates, "expert", axis=0, tiled=True)
    grad_all = (grad_all.astype(F32) * gate_of(routing_all, gates_all, expert)).astype(BF16)
    wg, wu, wd = w_gate[0], w_up[0], w_down[0]
    hid, dg, du = hidden_grads(dot(acts_all, wg, 1, 0), dot(acts_all, wu, 1, 0), dot(grad_all, wd, 1, 1))
    partial = dot(dg, wg, 1, 1) + dot(du, wu, 1, 1)
    partial = lax.psum_scatter(partial, "tensor", scatter_dimension=1, tiled=True)
    back = lax.psum_scatter(partial, "expert", scatter_dimension=0, tiled=True)
    return (
        dot(acts_all, dg, 0, 0).astype(BF16)[None],
        dot(acts_all, du, 0, 0).astype(BF16)[None],
        dot(hid, grad_all, 0, 0).astype(BF16)[None],
        back.astype(BF16),
    )


def solution(mesh):
    chips = mesh.shape["tensor"] == 8
    return jax.shard_map(
        chips_body if chips else any_body,
        mesh=mesh,
        in_specs=(
            P("expert", "tensor"),
            P("expert", "tensor"),
            P("expert", None),
            P("expert", None),
            P("expert", None, "tensor"),
            P("expert", None, "tensor"),
            P("expert", "tensor", None),
        ),
        out_specs=(
            P("expert", None, "tensor"),
            P("expert", None, "tensor"),
            P("expert", "tensor", None),
            P("expert", "tensor"),
        ),
        check_vma=False,
    )
```

```python
import functools

import jax
import jax.numpy as jnp
from jax import lax
from jax.experimental import pallas as pl
from jax.experimental.pallas import tpu as pltpu
from jax.sharding import PartitionSpec as P

F32 = jnp.float32
BF16 = jnp.bfloat16


def dot(left, right, left_dim, right_dim):
    return lax.dot_general(
        left, right, (((left_dim,), (right_dim,)), ((), ())), preferred_element_type=F32
    )


def gate_of(routing, gates, expert):
    return jnp.sum(jnp.where(routing == expert, gates, 0.0), axis=1, keepdims=True)


def hidden_grads(gate_pre, up_pre, grad_hidden):
    sig = jax.nn.sigmoid(gate_pre)
    act = gate_pre * sig
    hidden = (act * up_pre).astype(BF16)
    grad_up_pre = (grad_hidden * act).astype(BF16)
    grad_gate_pre = (grad_hidden * up_pre * sig * (1.0 + gate_pre * (1.0 - sig))).astype(BF16)
    return hidden, grad_gate_pre, grad_up_pre


VMEM = pl.BlockSpec(memory_space=pltpu.VMEM)
SMEM = pl.BlockSpec(memory_space=pltpu.SMEM)
HBM = pl.BlockSpec(memory_space=pl.ANY)


def in_hbm(array):
    return pltpu.with_memory_space_constraint(array, pltpu.HBM)


def shape(dims, dtype):
    return jax.ShapeDtypeStruct(dims, dtype)


def call(kernel, out_shape, in_specs, out_specs, flops, moved, scratch=(), limit=8, aliases={}):
    return pl.pallas_call(
        kernel,
        out_shape=out_shape,
        in_specs=in_specs,
        out_specs=out_specs,
        scratch_shapes=scratch,
        input_output_aliases=aliases,
        compiler_params=pltpu.CompilerParams(vmem_limit_bytes=limit * 1024 * 1024),
        cost_estimate=pl.CostEstimate(flops=flops, bytes_accessed=moved, transcendentals=0),
    )


def both_cores(core, mine, other):
    first = core == 0
    return jnp.concatenate([jnp.where(first, mine, other), jnp.where(first, other, mine)], axis=1)


def block_at(place, p, wide):
    return pl.ds(pl.multiple_of((place[0] // 2 ^ p) * wide, wide), wide)


STEP = 256
LOAD_LIMIT = 28
PARTS = 2


def far(place):
    core = place[0] % 2
    return 0, 1 + core, 2 - core, 3


def pair(place, i, own, sib):
    core = place[0] % 2
    rows = block_at(place, far(place)[i], 2 * own.shape[2])
    return rows, both_cores(core, own[0], sib[0]), both_cores(core, own[1], sib[1])


def add_pieces(pieces, weights, acc_in, acc_out, finish):
    wg, wu, wd = weights
    for f in range(wg.shape[1] // STEP):
        cols = pl.ds(f * STEP, STEP)
        sums = [None if acc is None else acc[:, cols] for acc in acc_in]
        for rows, x, g in pieces:
            terms = (dot(x, wg[rows, cols], 1, 0), dot(x, wu[rows, cols], 1, 0), dot(g, wd[cols, rows], 1, 1))
            sums = [t if s is None else s + t for s, t in zip(sums, terms)]
        finish(cols, sums, acc_out)


def store(cols, sums, outs):
    for out, value in zip(outs, sums):
        out[:, cols] = value


def store_grads(cols, sums, outs):
    store(cols, hidden_grads(*sums), outs)


def turn(block, out):
    for c in range(0, block.shape[1], STEP):
        out[c : c + STEP, :] = block[:, c : c + STEP].T


def load_gate_kernel(place, source, here, turned, sems):
    wide = turned.shape[2]
    blocks = [block_at(place, p, wide) for p in range(4)]
    copies = [pltpu.make_async_copy(source.at[b, :], here.at[b, :], sems.at[p]) for p, b in enumerate(blocks)]
    for copy in copies:
        copy.start()
    for p, block in enumerate(blocks):
        copies[p].wait()
        turn(here[block, :], turned.at[p])


def load_gate(place, wg):
    full, hidden_count = wg.shape
    return call(
        load_gate_kernel,
        (shape(wg.shape, BF16), shape((4, hidden_count, full // 4), BF16)),
        [SMEM, HBM],
        [VMEM] * 2,
        1,
        1,
        scratch=[pltpu.SemaphoreType.DMA((4,))],
        limit=8,
    )(place, in_hbm(wg))


def load_up_kernel(place, own, near, source, wg, here, gate, up, turned, sems):
    row, x, _ = pair(place, 0, own, near)
    wide = x.shape[1]
    copies = []
    for p in range(4):
        rows = block_at(place, p, wide)
        copies.append(pltpu.make_async_copy(source.at[rows, :], here.at[rows, :], sems.at[p]))
        copies[p].start()
    for weight, total in ((wg, gate), (here, up)):
        if weight is here:
            copies[0].wait()
        for f in range(weight.shape[1] // STEP):
            cols = pl.ds(f * STEP, STEP)
            total[:, cols] = dot(x, weight[row, cols], 1, 0)
    for p in range(4):
        if p > 0:
            copies[p].wait()
        turn(here[block_at(place, p, wide), :], turned.at[p])


def load_up(place, own, near, wu, wg):
    rows, hidden_count = own.shape[1], wu.shape[1]
    return call(
        load_up_kernel,
        (shape(wu.shape, BF16),)
        + (shape((rows, hidden_count), F32),) * 2
        + (shape((4, hidden_count, wu.shape[0] // 4), BF16),),
        [SMEM] + [VMEM] * 2 + [HBM] + [VMEM],
        [VMEM] * 4,
        1,
        1,
        scratch=[pltpu.SemaphoreType.DMA((4,))],
        limit=8,
    )(place, own, near, in_hbm(wu), wg)


def back_kernel(place, own, near, wd, back, turned):
    row, _, g = pair(place, 0, own, near)
    for f in range(wd.shape[0] // STEP):
        cols = pl.ds(f * STEP, STEP)
        back[:, cols] = dot(g, wd[cols, row], 1, 1)
        for i in range(2):
            turned[i, :, cols] = wd[cols, block_at(place, far(place)[2 + i], g.shape[1])].T


def own_back(place, own, near, wd):
    rows, (hidden_count, full) = own.shape[1], wd.shape
    return call(
        back_kernel,
        (shape((rows, hidden_count), F32), shape((2, full // 4, hidden_count), BF16)),
        [SMEM] + [VMEM] * 3,
        [VMEM] * 2,
        1,
        1,
    )(place, own, near, wd)


def partial_kernel(place, own, sib, wg, wu, wd, *refs):
    add_pieces([pair(place, 1, own, sib)], (wg, wu, wd), refs[:3], refs[3:], store)


def partial_sums(place, own, sib, weights, acc):
    return call(
        partial_kernel,
        (shape(acc[0].shape, F32),) * 3,
        [SMEM] + [VMEM] * 8,
        [VMEM] * 3,
        1,
        1,
        aliases={6: 0, 7: 1, 8: 2},
    )(place, own, sib, *weights, *acc)


def third_kernel(place, own, sib, wg, wu, wd, gate_in, up_in, back_in, gate, up, back):
    rows, x, g = pair(place, 2, own, sib)
    for f in range(wg.shape[1] // STEP):
        cols = pl.ds(f * STEP, STEP)
        gate[:, cols] = gate_in[:, cols] + dot(x, wg[rows, cols], 1, 0)
        up[:, cols] = up_in[:, cols] + dot(x, wu[rows, cols], 1, 0)
        back[:, cols] = back_in[:, cols] + dot(g, wd[0, :, cols], 1, 0)


def third_sums(place, own, sib, weights, acc):
    return call(
        third_kernel,
        (shape(acc[0].shape, F32),) * 3,
        [SMEM] + [VMEM] * 8,
        [VMEM] * 3,
        1,
        1,
        aliases={6: 0, 7: 1, 8: 2},
    )(place, own, sib, *weights, *acc)


def write_slots(place, p, dg, du, wg, wu, keep, send):
    width = keep.shape[1]
    first = place[0] % 2 == 0
    part = dot(dg[...], wg[p], 1, 0) + dot(du[...], wu[p], 1, 0)
    low, high = part[:, :width], part[:, width:]
    keep[...] = jnp.where(first, low, high)
    send[...] = jnp.where(first, high, low).astype(BF16)


def middle_kernel(place, own, sib, wg, wu, wd, gate, up, back, hid, dg, du, keep, send):
    rows, x, g = pair(place, 3, own, sib)
    for f in range(wd.shape[2] // STEP):
        cols = pl.ds(f * STEP, STEP)
        sums = (
            gate[:, cols] + dot(x, wg[3, cols, :], 1, 1),
            up[:, cols] + dot(x, wu[3, cols, :], 1, 1),
            back[:, cols] + dot(g, wd[1, :, cols], 1, 0),
        )
        store_grads(cols, sums, (hid, dg, du))
    write_slots(place, 3, dg, du, wg, wu, keep, send)


def middle(place, own, sib, turned, wd, acc):
    rows, width = own.shape[1:]
    hidden_count = wd.shape[2]
    return call(
        middle_kernel,
        (shape((rows, hidden_count), BF16),) * 3 + (shape((rows, width), F32), shape((rows, width), BF16)),
        [SMEM] + [VMEM] * 8,
        [VMEM] * 5,
        20 * rows * width * hidden_count,
        0,
    )(place, own, sib, *turned, wd, *acc)


def slot_kernel(p, place, *refs):
    write_slots(place, p, *refs)


def slots(place, p, dg, du, turned):
    rows, hidden_count = dg.shape
    width = turned[1].shape[2] // 2
    return call(
        functools.partial(slot_kernel, p),
        (shape((rows, width), F32), shape((rows, width), BF16)),
        [SMEM] + [VMEM] * 4,
        [VMEM] * 2,
        8 * rows * width * hidden_count,
        0,
    )(place, dg, du, *turned)


def weight_kernel(jobs, begun, place, *refs):
    n = len(jobs)
    own, sib, ds = refs[0:4], refs[4:8], refs[8 : 8 + n]
    refs = refs[8 + n + begun :]
    outs, bufs, sems = refs[:n], refs[n : 2 * n], refs[2 * n]
    core = place[0] % 2
    wide = 2 * own[0].shape[2]
    chips = far(place)
    copies = []
    for i, ((array, pieces), d, out, buf) in enumerate(zip(jobs, ds, outs, bufs)):
        for j, p in enumerate(pieces):
            rows = block_at(place, chips[p], wide)
            piece = both_cores(core, own[p][array], sib[p][array])
            left, right = (piece, d[...]) if array == 0 else (d[...], piece)
            size = left.shape[1] // PARTS
            for k in range(PARTS):
                part = pl.ds(k * size, size)
                buf[j, part, :] = dot(left[:, k * size : (k + 1) * size], right, 0, 0).astype(BF16)
                if array == 0:
                    start = pl.multiple_of((place[0] // 2 ^ chips[p]) * wide + k * size, size)
                    target = out.at[pl.ds(start, size), :]
                else:
                    target = out.at[part, rows]
                copies.append(pltpu.make_async_copy(buf.at[j, part, :], target, sems.at[i, j, k]))
                copies[-1].start()
    for copy in copies:
        copy.wait()


def weight_grads(place, jobs, own, sib, ds, begun=None):
    rows, width = own[0].shape[1:]
    hidden_count = ds[0].shape[1]
    blocks = [(2 * width, hidden_count) if array == 0 else (hidden_count, 2 * width) for array, _ in jobs]
    outs = [(8 * width, hidden_count) if array == 0 else (hidden_count, 8 * width) for array, _ in jobs]
    count = sum(len(pieces) for _, pieces in jobs)
    more = [] if begun is None else [begun]
    return call(
        functools.partial(weight_kernel, jobs, len(more)),
        tuple(shape(out, BF16) for out in outs),
        [SMEM] + [VMEM] * (8 + len(ds)) + [HBM] * len(more),
        [HBM] * len(ds),
        4 * rows * width * hidden_count * count,
        4 * width * hidden_count * count,
        scratch=[pltpu.VMEM((len(pieces),) + block, BF16) for block, (_, pieces) in zip(blocks, jobs)]
        + [pltpu.SemaphoreType.DMA((len(ds), 4, PARTS))],
        limit=LOAD_LIMIT,
        aliases={9 + len(ds): 0} if more else {},
    )(place, *own, *sib, *ds, *more)


def pack_kernel(groups, place, *refs):
    sources, outs, here, sems = refs[:4], refs[4 : 4 + groups], refs[4 + groups : 8 + groups], refs[8 + groups]
    copies = [pltpu.make_async_copy(s, d, sems.at[i]) for i, (s, d) in enumerate(zip(sources, here))]
    for copy in copies:
        copy.start()
    for copy in copies:
        copy.wait()
    acts, grad, routing, gates = here
    wide = grad[...].astype(F32)
    for distance, out in enumerate(outs):
        expert = lax.rem(place[0] + distance, groups)
        gate = jnp.sum(jnp.where(routing[...] == expert, gates[...], 0.0), axis=0, keepdims=True)
        out[0] = acts[...]
        out[1] = (wide * gate.T).astype(BF16)


def pack(place, acts, grad, routing, gates, groups):
    sources = tuple(in_hbm(s) for s in (acts, grad, routing.T, gates.T))
    return call(
        functools.partial(pack_kernel, groups),
        (shape((2,) + acts.shape, BF16),) * groups,
        [SMEM] + [HBM] * 4,
        [VMEM] * groups,
        1,
        1,
        scratch=[pltpu.VMEM(s.shape, s.dtype) for s in sources] + [pltpu.SemaphoreType.DMA((4,))],
        limit=16,
    )(place, *sources)


def across(array, even, odd=None):
    masks = (even, even if odd is None else odd)
    return lax.ppermute(array, "tensor", [(i, i ^ masks[i % 2]) for i in range(8)])


def along(array, distance, count):
    return lax.ppermute(array, "expert", [(i, (i + distance) % count) for i in range(count)])


def chips_body(acts, grad_out, routing, gates, w_gate, w_up, w_down):
    groups = lax.axis_size("expert")
    place = lax.axis_index("tensor").astype(jnp.int32)[None]
    z = lax.axis_index("expert").astype(jnp.int32)[None]
    tok_count, width = acts.shape
    packed = pack(z, acts, grad_out, routing, gates, groups)
    blocks = [along(packed[k], k, groups) for k in range(1, groups)]
    wg, wg_turned = load_gate(place, w_gate[0])
    blocks, wg, wg_turned = lax.optimization_barrier((blocks, wg, wg_turned))
    own = jnp.concatenate([packed[0]] + blocks, axis=1)
    near = across(own, 1)
    here = across(own, 2, 4), across(near, 2, 4)
    wu, gate, up, wu_turned = load_up(place, own, near, w_up[0], wg)
    first, gate, up = lax.optimization_barrier((here[0], gate, up))
    diag = across(first, 4, 2)
    there_second = across(first, 1)
    wd = w_down[0]
    back, wd_turned = own_back(place, own, near, wd)
    second, back = lax.optimization_barrier((here[1], back))
    there_first = across(second, 1)
    weights, acc = (wg, wu, wd), (gate, up, back)
    acc = partial_sums(place, first, second, weights, acc)
    turned = wg_turned, wu_turned
    diag, acc = lax.optimization_barrier((diag, acc))
    diag_near = across(diag, 1)
    acc = third_sums(place, there_first, there_second, (wg, wu, wd_turned), acc)
    hid, dg, du, keep, send = middle(place, diag, diag_near, turned, wd_turned, acc)
    mine_of = own, first, there_first, diag
    other_of = near, second, there_second, diag_near

    def chip_sum(keep, send):
        return keep + across(send, 1).astype(F32)

    shares = {1: slots(place, 1, dg, du, turned)}
    total, dg, du = lax.optimization_barrier((chip_sum(keep, send), dg, du))
    parts = [across(total.astype(BF16), 6)]
    shares[2] = slots(place, 2, dg, du, turned)
    parts.append(across(chip_sum(*shares[1]).astype(BF16), 2))
    total, dg, du = lax.optimization_barrier((chip_sum(*shares[2]), dg, du))
    parts.append(across(total.astype(BF16), 4))
    share = slots(place, 0, dg, du, turned)
    share, dg = lax.optimization_barrier((share, dg))
    (grad_gate,) = weight_grads(place, [(0, (0, 1))], mine_of, other_of, (dg,))
    mine = chip_sum(*share)
    parts[0], dg, grad_gate = lax.optimization_barrier((parts[0], dg, grad_gate))
    (grad_gate,) = weight_grads(place, [(0, (2, 3))], mine_of, other_of, (dg,), grad_gate)
    for part in parts:
        mine = mine + part.astype(F32)
    mine, hid, grad_gate = lax.optimization_barrier((mine, hid, grad_gate))
    whole = (0, 1, 2, 3)
    grad_up, grad_down = weight_grads(place, [(0, whole), (1, whole)], mine_of, other_of, (du, hid))
    mine = mine.reshape(groups, tok_count, width)
    back = mine[0]
    sent = mine.astype(BF16)
    for k in range(1, groups):
        back = back + along(sent[k], -k, groups).astype(F32)
    return (grad_gate[None], grad_up[None], grad_down[None], back.astype(BF16))


def any_body(acts, grad_out, routing, gates, w_gate, w_up, w_down):
    expert = lax.axis_index("expert")
    acts_all, grad_all = (
        lax.all_gather(
            lax.all_gather(array, "tensor", axis=1, tiled=True), "expert", axis=0, tiled=True
        )
        for array in (acts, grad_out)
    )
    routing_all = lax.all_gather(routing, "expert", axis=0, tiled=True)
    gates_all = lax.all_gather(gates, "expert", axis=0, tiled=True)
    grad_all = (grad_all.astype(F32) * gate_of(routing_all, gates_all, expert)).astype(BF16)
    wg, wu, wd = w_gate[0], w_up[0], w_down[0]
    hid, dg, du = hidden_grads(dot(acts_all, wg, 1, 0), dot(acts_all, wu, 1, 0), dot(grad_all, wd, 1, 1))
    partial = dot(dg, wg, 1, 1) + dot(du, wu, 1, 1)
    partial = lax.psum_scatter(partial, "tensor", scatter_dimension=1, tiled=True)
    back = lax.psum_scatter(partial, "expert", scatter_dimension=0, tiled=True)
    return (
        dot(acts_all, dg, 0, 0).astype(BF16)[None],
        dot(acts_all, du, 0, 0).astype(BF16)[None],
        dot(hid, grad_all, 0, 0).astype(BF16)[None],
        back.astype(BF16),
    )


def solution(mesh):
    chips = mesh.shape["tensor"] == 8
    return jax.shard_map(
        chips_body if chips else any_body,
        mesh=mesh,
        in_specs=(
            P("expert", "tensor"),
            P("expert", "tensor"),
            P("expert", None),
            P("expert", None),
            P("expert", None, "tensor"),
            P("expert", None, "tensor"),
            P("expert", "tensor", None),
        ),
        out_specs=(
            P("expert", None, "tensor"),
            P("expert", None, "tensor"),
            P("expert", "tensor", None),
            P("expert", "tensor"),
        ),
        check_vma=False,
    )
```

```python
import functools

import jax
import jax.numpy as jnp
from jax import lax
from jax.experimental import pallas as pl
from jax.experimental.pallas import tpu as pltpu
from jax.sharding import PartitionSpec as P

F32 = jnp.float32
BF16 = jnp.bfloat16


def dot(left, right, left_dim, right_dim):
    return lax.dot_general(
        left, right, (((left_dim,), (right_dim,)), ((), ())), preferred_element_type=F32
    )


def gate_of(routing, gates, expert):
    return jnp.sum(jnp.where(routing == expert, gates, 0.0), axis=1, keepdims=True)


def hidden_grads(gate_pre, up_pre, grad_hidden):
    sig = jax.nn.sigmoid(gate_pre)
    act = gate_pre * sig
    hidden = (act * up_pre).astype(BF16)
    grad_up_pre = (grad_hidden * act).astype(BF16)
    grad_gate_pre = (grad_hidden * up_pre * sig * (1.0 + gate_pre * (1.0 - sig))).astype(BF16)
    return hidden, grad_gate_pre, grad_up_pre


VMEM = pl.BlockSpec(memory_space=pltpu.VMEM)
SMEM = pl.BlockSpec(memory_space=pltpu.SMEM)
HBM = pl.BlockSpec(memory_space=pl.ANY)


def in_hbm(array):
    return pltpu.with_memory_space_constraint(array, pltpu.HBM)


def shape(dims, dtype):
    return jax.ShapeDtypeStruct(dims, dtype)


def call(kernel, out_shape, in_specs, out_specs, flops, moved, scratch=(), limit=8, aliases={}):
    return pl.pallas_call(
        kernel,
        out_shape=out_shape,
        in_specs=in_specs,
        out_specs=out_specs,
        scratch_shapes=scratch,
        input_output_aliases=aliases,
        compiler_params=pltpu.CompilerParams(vmem_limit_bytes=limit * 1024 * 1024),
        cost_estimate=pl.CostEstimate(flops=flops, bytes_accessed=moved, transcendentals=0),
    )


def both_cores(core, mine, other):
    first = core == 0
    return jnp.concatenate([jnp.where(first, mine, other), jnp.where(first, other, mine)], axis=1)


def block_at(place, p, wide):
    return pl.ds(pl.multiple_of((place[0] // 2 ^ p) * wide, wide), wide)


STEP = 256
LOAD_LIMIT = 28
PARTS = 2


def far(place):
    core = place[0] % 2
    return 0, 1 + core, 2 - core, 3


def pair(place, i, own, sib):
    core = place[0] % 2
    rows = block_at(place, far(place)[i], 2 * own.shape[2])
    return rows, both_cores(core, own[0], sib[0]), both_cores(core, own[1], sib[1])


def add_pieces(pieces, weights, acc_in, acc_out, finish):
    wg, wu, wd = weights
    for f in range(wg.shape[1] // STEP):
        cols = pl.ds(f * STEP, STEP)
        sums = [None if acc is None else acc[:, cols] for acc in acc_in]
        for rows, x, g in pieces:
            terms = (dot(x, wg[rows, cols], 1, 0), dot(x, wu[rows, cols], 1, 0), dot(g, wd[cols, rows], 1, 1))
            sums = [t if s is None else s + t for s, t in zip(sums, terms)]
        finish(cols, sums, acc_out)


def store(cols, sums, outs):
    for out, value in zip(outs, sums):
        out[:, cols] = value


def store_grads(cols, sums, outs):
    store(cols, hidden_grads(*sums), outs)


def turn(block, out):
    for c in range(0, block.shape[1], STEP):
        out[c : c + STEP, :] = block[:, c : c + STEP].T


def load_gate_kernel(place, source, here, turned, sems):
    wide = turned.shape[2]
    blocks = [block_at(place, p, wide) for p in range(4)]
    copies = [pltpu.make_async_copy(source.at[b, :], here.at[b, :], sems.at[p]) for p, b in enumerate(blocks)]
    for copy in copies:
        copy.start()
    for p, block in enumerate(blocks):
        copies[p].wait()
        turn(here[block, :], turned.at[p])


def load_gate(place, wg):
    full, hidden_count = wg.shape
    return call(
        load_gate_kernel,
        (shape(wg.shape, BF16), shape((4, hidden_count, full // 4), BF16)),
        [SMEM, HBM],
        [VMEM] * 2,
        1,
        1,
        scratch=[pltpu.SemaphoreType.DMA((4,))],
        limit=8,
    )(place, in_hbm(wg))


def load_up_kernel(place, own, near, source, wg, here, gate, up, turned, sems):
    row, x, _ = pair(place, 0, own, near)
    wide = x.shape[1]
    copies = []
    for p in range(4):
        rows = block_at(place, p, wide)
        copies.append(pltpu.make_async_copy(source.at[rows, :], here.at[rows, :], sems.at[p]))
        copies[p].start()
    for weight, total in ((wg, gate), (here, up)):
        if weight is here:
            copies[0].wait()
        for f in range(weight.shape[1] // STEP):
            cols = pl.ds(f * STEP, STEP)
            total[:, cols] = dot(x, weight[row, cols], 1, 0)
    for p in range(4):
        if p > 0:
            copies[p].wait()
        turn(here[block_at(place, p, wide), :], turned.at[p])


def load_up(place, own, near, wu, wg):
    rows, hidden_count = own.shape[1], wu.shape[1]
    return call(
        load_up_kernel,
        (shape(wu.shape, BF16),)
        + (shape((rows, hidden_count), F32),) * 2
        + (shape((4, hidden_count, wu.shape[0] // 4), BF16),),
        [SMEM] + [VMEM] * 2 + [HBM] + [VMEM],
        [VMEM] * 4,
        1,
        1,
        scratch=[pltpu.SemaphoreType.DMA((4,))],
        limit=8,
    )(place, own, near, in_hbm(wu), wg)


def back_kernel(place, own, near, wd, back, turned):
    row, _, g = pair(place, 0, own, near)
    for f in range(wd.shape[0] // STEP):
        cols = pl.ds(f * STEP, STEP)
        back[:, cols] = dot(g, wd[cols, row], 1, 1)
        for i in range(2):
            turned[i, :, cols] = wd[cols, block_at(place, far(place)[2 + i], g.shape[1])].T


def own_back(place, own, near, wd):
    rows, (hidden_count, full) = own.shape[1], wd.shape
    return call(
        back_kernel,
        (shape((rows, hidden_count), F32), shape((2, full // 4, hidden_count), BF16)),
        [SMEM] + [VMEM] * 3,
        [VMEM] * 2,
        1,
        1,
    )(place, own, near, wd)


def partial_kernel(place, own, sib, wg, wu, wd, *refs):
    add_pieces([pair(place, 1, own, sib)], (wg, wu, wd), refs[:3], refs[3:], store)


def partial_sums(place, own, sib, weights, acc):
    return call(
        partial_kernel,
        (shape(acc[0].shape, F32),) * 3,
        [SMEM] + [VMEM] * 8,
        [VMEM] * 3,
        1,
        1,
        aliases={6: 0, 7: 1, 8: 2},
    )(place, own, sib, *weights, *acc)


def third_kernel(place, own, sib, wg, wu, wd, gate_in, up_in, back_in, gate, up, back):
    rows, x, g = pair(place, 2, own, sib)
    for f in range(wg.shape[1] // STEP):
        cols = pl.ds(f * STEP, STEP)
        gate[:, cols] = gate_in[:, cols] + dot(x, wg[rows, cols], 1, 0)
        up[:, cols] = up_in[:, cols] + dot(x, wu[rows, cols], 1, 0)
        back[:, cols] = back_in[:, cols] + dot(g, wd[0, :, cols], 1, 0)


def third_sums(place, own, sib, weights, acc):
    return call(
        third_kernel,
        (shape(acc[0].shape, F32),) * 3,
        [SMEM] + [VMEM] * 8,
        [VMEM] * 3,
        1,
        1,
        aliases={6: 0, 7: 1, 8: 2},
    )(place, own, sib, *weights, *acc)


def write_slots(place, p, dg, du, wg, wu, keep, send):
    width = keep.shape[1]
    first = place[0] % 2 == 0
    part = dot(dg[...], wg[p], 1, 0) + dot(du[...], wu[p], 1, 0)
    low, high = part[:, :width], part[:, width:]
    keep[...] = jnp.where(first, low, high)
    send[...] = jnp.where(first, high, low).astype(BF16)


def middle_kernel(place, own, sib, wg, wu, wd, wg_turned, wu_turned, gate, up, back, hid, dg, du, keep, send):
    rows, x, g = pair(place, 3, own, sib)
    for f in range(wd.shape[2] // STEP):
        cols = pl.ds(f * STEP, STEP)
        sums = (
            gate[:, cols] + dot(x, wg[rows, cols], 1, 0),
            up[:, cols] + dot(x, wu[rows, cols], 1, 0),
            back[:, cols] + dot(g, wd[1, :, cols], 1, 0),
        )
        store_grads(cols, sums, (hid, dg, du))
    write_slots(place, 3, dg, du, wg_turned, wu_turned, keep, send)


def middle(place, own, sib, weights, turned, acc):
    rows, width = own.shape[1:]
    hidden_count = turned[0].shape[1]
    return call(
        middle_kernel,
        (shape((rows, hidden_count), BF16),) * 3 + (shape((rows, width), F32), shape((rows, width), BF16)),
        [SMEM] + [VMEM] * 10,
        [VMEM] * 5,
        20 * rows * width * hidden_count,
        0,
    )(place, own, sib, *weights, *turned, *acc)


def slot_kernel(p, place, *refs):
    write_slots(place, p, *refs)


def slots(place, p, dg, du, turned):
    rows, hidden_count = dg.shape
    width = turned[1].shape[2] // 2
    return call(
        functools.partial(slot_kernel, p),
        (shape((rows, width), F32), shape((rows, width), BF16)),
        [SMEM] + [VMEM] * 4,
        [VMEM] * 2,
        8 * rows * width * hidden_count,
        0,
    )(place, dg, du, *turned)


def weight_kernel(jobs, begun, place, *refs):
    n = len(jobs)
    own, sib, ds = refs[0:4], refs[4:8], refs[8 : 8 + n]
    refs = refs[8 + n + begun :]
    outs, bufs, sems = refs[:n], refs[n : 2 * n], refs[2 * n]
    core = place[0] % 2
    wide = 2 * own[0].shape[2]
    chips = far(place)
    copies = []
    for i, ((array, pieces), d, out, buf) in enumerate(zip(jobs, ds, outs, bufs)):
        for j, p in enumerate(pieces):
            rows = block_at(place, chips[p], wide)
            piece = both_cores(core, own[p][array], sib[p][array])
            left, right = (piece, d[...]) if array == 0 else (d[...], piece)
            size = left.shape[1] // PARTS
            for k in range(PARTS):
                part = pl.ds(k * size, size)
                buf[j, part, :] = dot(left[:, k * size : (k + 1) * size], right, 0, 0).astype(BF16)
                if array == 0:
                    start = pl.multiple_of((place[0] // 2 ^ chips[p]) * wide + k * size, size)
                    target = out.at[pl.ds(start, size), :]
                else:
                    target = out.at[part, rows]
                copies.append(pltpu.make_async_copy(buf.at[j, part, :], target, sems.at[i, j, k]))
                copies[-1].start()
    for copy in copies:
        copy.wait()


def weight_grads(place, jobs, own, sib, ds, begun=None):
    rows, width = own[0].shape[1:]
    hidden_count = ds[0].shape[1]
    blocks = [(2 * width, hidden_count) if array == 0 else (hidden_count, 2 * width) for array, _ in jobs]
    outs = [(8 * width, hidden_count) if array == 0 else (hidden_count, 8 * width) for array, _ in jobs]
    count = sum(len(pieces) for _, pieces in jobs)
    more = [] if begun is None else [begun]
    return call(
        functools.partial(weight_kernel, jobs, len(more)),
        tuple(shape(out, BF16) for out in outs),
        [SMEM] + [VMEM] * (8 + len(ds)) + [HBM] * len(more),
        [HBM] * len(ds),
        4 * rows * width * hidden_count * count,
        4 * width * hidden_count * count,
        scratch=[pltpu.VMEM((len(pieces),) + block, BF16) for block, (_, pieces) in zip(blocks, jobs)]
        + [pltpu.SemaphoreType.DMA((len(ds), 4, PARTS))],
        limit=LOAD_LIMIT,
        aliases={9 + len(ds): 0} if more else {},
    )(place, *own, *sib, *ds, *more)


def pack_kernel(groups, place, *refs):
    sources, outs, here, sems = refs[:4], refs[4 : 4 + groups], refs[4 + groups : 8 + groups], refs[8 + groups]
    copies = [pltpu.make_async_copy(s, d, sems.at[i]) for i, (s, d) in enumerate(zip(sources, here))]
    for copy in copies:
        copy.start()
    for copy in copies:
        copy.wait()
    acts, grad, routing, gates = here
    wide = grad[...].astype(F32)
    for distance, out in enumerate(outs):
        expert = lax.rem(place[0] + distance, groups)
        gate = jnp.sum(jnp.where(routing[...] == expert, gates[...], 0.0), axis=0, keepdims=True)
        out[0] = acts[...]
        out[1] = (wide * gate.T).astype(BF16)


def pack(place, acts, grad, routing, gates, groups):
    sources = tuple(in_hbm(s) for s in (acts, grad, routing.T, gates.T))
    return call(
        functools.partial(pack_kernel, groups),
        (shape((2,) + acts.shape, BF16),) * groups,
        [SMEM] + [HBM] * 4,
        [VMEM] * groups,
        1,
        1,
        scratch=[pltpu.VMEM(s.shape, s.dtype) for s in sources] + [pltpu.SemaphoreType.DMA((4,))],
        limit=16,
    )(place, *sources)


def across(array, even, odd=None):
    masks = (even, even if odd is None else odd)
    return lax.ppermute(array, "tensor", [(i, i ^ masks[i % 2]) for i in range(8)])


def along(array, distance, count):
    return lax.ppermute(array, "expert", [(i, (i + distance) % count) for i in range(count)])


def chips_body(acts, grad_out, routing, gates, w_gate, w_up, w_down):
    groups = lax.axis_size("expert")
    place = lax.axis_index("tensor").astype(jnp.int32)[None]
    z = lax.axis_index("expert").astype(jnp.int32)[None]
    tok_count, width = acts.shape
    packed = pack(z, acts, grad_out, routing, gates, groups)
    blocks = [along(packed[k], k, groups) for k in range(1, groups)]
    wg, wg_turned = load_gate(place, w_gate[0])
    blocks, wg, wg_turned = lax.optimization_barrier((blocks, wg, wg_turned))
    own = jnp.concatenate([packed[0]] + blocks, axis=1)
    near = across(own, 1)
    here = across(own, 2, 4), across(near, 2, 4)
    wu, gate, up, wu_turned = load_up(place, own, near, w_up[0], wg)
    first, gate, up = lax.optimization_barrier((here[0], gate, up))
    diag = across(first, 4, 2)
    there_second = across(first, 1)
    wd = w_down[0]
    back, wd_turned = own_back(place, own, near, wd)
    second, back = lax.optimization_barrier((here[1], back))
    there_first = across(second, 1)
    weights, acc = (wg, wu, wd), (gate, up, back)
    acc = partial_sums(place, first, second, weights, acc)
    turned = wg_turned, wu_turned
    diag, acc = lax.optimization_barrier((diag, acc))
    diag_near = across(diag, 1)
    acc = third_sums(place, there_first, there_second, (wg, wu, wd_turned), acc)
    hid, dg, du, keep, send = middle(place, diag, diag_near, (wg, wu, wd_turned), turned, acc)
    mine_of = own, first, there_first, diag
    other_of = near, second, there_second, diag_near

    def chip_sum(keep, send):
        return keep + across(send, 1).astype(F32)

    shares = {1: slots(place, 1, dg, du, turned)}
    total, dg, du = lax.optimization_barrier((chip_sum(keep, send), dg, du))
    parts = [across(total.astype(BF16), 6)]
    shares[2] = slots(place, 2, dg, du, turned)
    parts.append(across(chip_sum(*shares[1]).astype(BF16), 2))
    total, dg, du = lax.optimization_barrier((chip_sum(*shares[2]), dg, du))
    parts.append(across(total.astype(BF16), 4))
    share = slots(place, 0, dg, du, turned)
    share, dg = lax.optimization_barrier((share, dg))
    (grad_gate,) = weight_grads(place, [(0, (0, 1))], mine_of, other_of, (dg,))
    mine = chip_sum(*share)
    parts[0], dg, grad_gate = lax.optimization_barrier((parts[0], dg, grad_gate))
    (grad_gate,) = weight_grads(place, [(0, (2, 3))], mine_of, other_of, (dg,), grad_gate)
    for part in parts:
        mine = mine + part.astype(F32)
    mine, hid, grad_gate = lax.optimization_barrier((mine, hid, grad_gate))
    whole = (0, 1, 2, 3)
    grad_up, grad_down = weight_grads(place, [(0, whole), (1, whole)], mine_of, other_of, (du, hid))
    mine = mine.reshape(groups, tok_count, width)
    back = mine[0]
    sent = mine.astype(BF16)
    for k in range(1, groups):
        back = back + along(sent[k], -k, groups).astype(F32)
    return (grad_gate[None], grad_up[None], grad_down[None], back.astype(BF16))


def any_body(acts, grad_out, routing, gates, w_gate, w_up, w_down):
    expert = lax.axis_index("expert")
    acts_all, grad_all = (
        lax.all_gather(
            lax.all_gather(array, "tensor", axis=1, tiled=True), "expert", axis=0, tiled=True
        )
        for array in (acts, grad_out)
    )
    routing_all = lax.all_gather(routing, "expert", axis=0, tiled=True)
    gates_all = lax.all_gather(gates, "expert", axis=0, tiled=True)
    grad_all = (grad_all.astype(F32) * gate_of(routing_all, gates_all, expert)).astype(BF16)
    wg, wu, wd = w_gate[0], w_up[0], w_down[0]
    hid, dg, du = hidden_grads(dot(acts_all, wg, 1, 0), dot(acts_all, wu, 1, 0), dot(grad_all, wd, 1, 1))
    partial = dot(dg, wg, 1, 1) + dot(du, wu, 1, 1)
    partial = lax.psum_scatter(partial, "tensor", scatter_dimension=1, tiled=True)
    back = lax.psum_scatter(partial, "expert", scatter_dimension=0, tiled=True)
    return (
        dot(acts_all, dg, 0, 0).astype(BF16)[None],
        dot(acts_all, du, 0, 0).astype(BF16)[None],
        dot(hid, grad_all, 0, 0).astype(BF16)[None],
        back.astype(BF16),
    )


def solution(mesh):
    chips = mesh.shape["tensor"] == 8
    return jax.shard_map(
        chips_body if chips else any_body,
        mesh=mesh,
        in_specs=(
            P("expert", "tensor"),
            P("expert", "tensor"),
            P("expert", None),
            P("expert", None),
            P("expert", None, "tensor"),
            P("expert", None, "tensor"),
            P("expert", "tensor", None),
        ),
        out_specs=(
            P("expert", None, "tensor"),
            P("expert", None, "tensor"),
            P("expert", "tensor", None),
            P("expert", "tensor"),
        ),
        check_vma=False,
    )
```

```python
import functools

import jax
import jax.numpy as jnp
from jax import lax
from jax.experimental import pallas as pl
from jax.experimental.pallas import tpu as pltpu
from jax.sharding import PartitionSpec as P

F32 = jnp.float32
BF16 = jnp.bfloat16


def dot(left, right, left_dim, right_dim):
    return lax.dot_general(
        left, right, (((left_dim,), (right_dim,)), ((), ())), preferred_element_type=F32
    )


def gate_of(routing, gates, expert):
    return jnp.sum(jnp.where(routing == expert, gates, 0.0), axis=1, keepdims=True)


def hidden_grads(gate_pre, up_pre, grad_hidden):
    sig = jax.nn.sigmoid(gate_pre)
    act = gate_pre * sig
    hidden = (act * up_pre).astype(BF16)
    grad_up_pre = (grad_hidden * act).astype(BF16)
    grad_gate_pre = (grad_hidden * up_pre * sig * (1.0 + gate_pre * (1.0 - sig))).astype(BF16)
    return hidden, grad_gate_pre, grad_up_pre


VMEM = pl.BlockSpec(memory_space=pltpu.VMEM)
SMEM = pl.BlockSpec(memory_space=pltpu.SMEM)
HBM = pl.BlockSpec(memory_space=pl.ANY)


def in_hbm(array):
    return pltpu.with_memory_space_constraint(array, pltpu.HBM)


def shape(dims, dtype):
    return jax.ShapeDtypeStruct(dims, dtype)


def call(kernel, out_shape, in_specs, out_specs, flops, moved, scratch=(), limit=8, aliases={}):
    return pl.pallas_call(
        kernel,
        out_shape=out_shape,
        in_specs=in_specs,
        out_specs=out_specs,
        scratch_shapes=scratch,
        input_output_aliases=aliases,
        compiler_params=pltpu.CompilerParams(vmem_limit_bytes=limit * 1024 * 1024),
        cost_estimate=pl.CostEstimate(flops=flops, bytes_accessed=moved, transcendentals=0),
    )


def both_cores(core, mine, other):
    first = core == 0
    return jnp.concatenate([jnp.where(first, mine, other), jnp.where(first, other, mine)], axis=1)


def block_at(place, p, wide):
    return pl.ds(pl.multiple_of((place[0] // 2 ^ p) * wide, wide), wide)


STEP = 256
LOAD_LIMIT = 28
PARTS = 2


def far(place):
    core = place[0] % 2
    return 0, 1 + core, 2 - core, 3


def pair(place, i, own, sib):
    core = place[0] % 2
    rows = block_at(place, far(place)[i], 2 * own.shape[2])
    return rows, both_cores(core, own[0], sib[0]), both_cores(core, own[1], sib[1])


def add_pieces(pieces, weights, acc_in, acc_out, finish):
    wg, wu, wd = weights
    for f in range(wg.shape[1] // STEP):
        cols = pl.ds(f * STEP, STEP)
        sums = [None if acc is None else acc[:, cols] for acc in acc_in]
        for rows, x, g in pieces:
            terms = (dot(x, wg[rows, cols], 1, 0), dot(x, wu[rows, cols], 1, 0), dot(g, wd[cols, rows], 1, 1))
            sums = [t if s is None else s + t for s, t in zip(sums, terms)]
        finish(cols, sums, acc_out)


def store(cols, sums, outs):
    for out, value in zip(outs, sums):
        out[:, cols] = value


def store_grads(cols, sums, outs):
    store(cols, hidden_grads(*sums), outs)


def turn(block, out):
    for c in range(0, block.shape[1], STEP):
        out[c : c + STEP, :] = block[:, c : c + STEP].T


def load_gate_kernel(place, source, here, turned, sems):
    wide = turned.shape[2]
    blocks = [block_at(place, p, wide) for p in range(4)]
    copies = [pltpu.make_async_copy(source.at[b, :], here.at[b, :], sems.at[p]) for p, b in enumerate(blocks)]
    for copy in copies:
        copy.start()
    for p, block in enumerate(blocks):
        copies[p].wait()
        turn(here[block, :], turned.at[p])


def load_gate(place, wg):
    full, hidden_count = wg.shape
    return call(
        load_gate_kernel,
        (shape(wg.shape, BF16), shape((4, hidden_count, full // 4), BF16)),
        [SMEM, HBM],
        [VMEM] * 2,
        1,
        1,
        scratch=[pltpu.SemaphoreType.DMA((4,))],
        limit=8,
    )(place, in_hbm(wg))


def load_up_kernel(place, own, near, source, wg, here, gate, up, turned, sems):
    row, x, _ = pair(place, 0, own, near)
    wide = x.shape[1]
    copies = []
    for p in range(4):
        rows = block_at(place, p, wide)
        copies.append(pltpu.make_async_copy(source.at[rows, :], here.at[rows, :], sems.at[p]))
        copies[p].start()
    for weight, total in ((wg, gate), (here, up)):
        if weight is here:
            copies[0].wait()
        for f in range(weight.shape[1] // STEP):
            cols = pl.ds(f * STEP, STEP)
            total[:, cols] = dot(x, weight[row, cols], 1, 0)
    for p in range(4):
        if p > 0:
            copies[p].wait()
        turn(here[block_at(place, p, wide), :], turned.at[p])


def load_up(place, own, near, wu, wg):
    rows, hidden_count = own.shape[1], wu.shape[1]
    return call(
        load_up_kernel,
        (shape(wu.shape, BF16),)
        + (shape((rows, hidden_count), F32),) * 2
        + (shape((4, hidden_count, wu.shape[0] // 4), BF16),),
        [SMEM] + [VMEM] * 2 + [HBM] + [VMEM],
        [VMEM] * 4,
        1,
        1,
        scratch=[pltpu.SemaphoreType.DMA((4,))],
        limit=8,
    )(place, own, near, in_hbm(wu), wg)


def back_kernel(place, own, near, wd, back, turned):
    row, _, g = pair(place, 0, own, near)
    for f in range(wd.shape[0] // STEP):
        cols = pl.ds(f * STEP, STEP)
        back[:, cols] = dot(g, wd[cols, row], 1, 1)
        for i in range(2):
            turned[i, :, cols] = wd[cols, block_at(place, far(place)[2 + i], g.shape[1])].T


def own_back(place, own, near, wd):
    rows, (hidden_count, full) = own.shape[1], wd.shape
    return call(
        back_kernel,
        (shape((rows, hidden_count), F32), shape((2, full // 4, hidden_count), BF16)),
        [SMEM] + [VMEM] * 3,
        [VMEM] * 2,
        1,
        1,
    )(place, own, near, wd)


def half_at(place, i, core, half, wg, wu, turned):
    x, g = half[0], half[1]
    width = x.shape[1]
    rows = (place[0] // 2 ^ far(place)[i]) * 2 * width + core * width
    rows = pl.ds(pl.multiple_of(rows, width), width)
    down = pl.ds(pl.multiple_of(core * width, width), width)

    def terms(cols):
        return dot(x, wg[rows, cols], 1, 0), dot(x, wu[rows, cols], 1, 0), dot(g, turned[i - 2, down, cols], 1, 0)

    return terms


def add_halves(halves, count, acc_in, finish, acc_out):
    for f in range(count // STEP):
        cols = pl.ds(f * STEP, STEP)
        sums = [acc[:, cols] for acc in acc_in]
        for terms in halves:
            sums = [s + t for s, t in zip(sums, terms(cols))]
        finish(cols, sums, acc_out)


def partial_kernel(place, own, sib, other, wg, wu, wd, turned, *refs):
    add_pieces([pair(place, 1, own, sib)], (wg, wu, wd), refs[:3], refs[3:], store)
    terms = half_at(place, 2, 1 - place[0] % 2, other, wg, wu, turned)
    add_halves([terms], wg.shape[1], refs[3:], store, refs[3:])


def partial_sums(place, own, sib, other, weights, turned, acc):
    return call(
        partial_kernel,
        (shape(acc[0].shape, F32),) * 3,
        [SMEM] + [VMEM] * 10,
        [VMEM] * 3,
        1,
        1,
        aliases={8: 0, 9: 1, 10: 2},
    )(place, own, sib, other, *weights, turned, *acc)


def third_kernel(place, rest, diag, wg, wu, turned, *refs):
    core = place[0] % 2
    halves = [half_at(place, i, core, half, wg, wu, turned) for i, half in ((2, rest), (3, diag))]
    add_halves(halves, wg.shape[1], refs[:3], store, refs[3:])


def third_sums(place, rest, diag, weights, acc):
    return call(
        third_kernel,
        (shape(acc[0].shape, F32),) * 3,
        [SMEM] + [VMEM] * 8,
        [VMEM] * 3,
        1,
        1,
        aliases={6: 0, 7: 1, 8: 2},
    )(place, rest, diag, *weights, *acc)


def write_slots(place, p, dg, du, wg, wu, keep, send):
    width = keep.shape[1]
    first = place[0] % 2 == 0
    part = dot(dg[...], wg[p], 1, 0) + dot(du[...], wu[p], 1, 0)
    low, high = part[:, :width], part[:, width:]
    keep[...] = jnp.where(first, low, high)
    send[...] = jnp.where(first, high, low).astype(BF16)


def middle_kernel(place, sib, wg, wu, turned, wg_turned, wu_turned, gate, up, back, hid, dg, du, keep, send):
    terms = half_at(place, 3, 1 - place[0] % 2, sib, wg, wu, turned)
    add_halves([terms], wg.shape[1], (gate, up, back), store_grads, (hid, dg, du))
    write_slots(place, 3, dg, du, wg_turned, wu_turned, keep, send)


def middle(place, sib, weights, turned, acc):
    rows, width = sib.shape[1:]
    hidden_count = turned[0].shape[1]
    return call(
        middle_kernel,
        (shape((rows, hidden_count), BF16),) * 3 + (shape((rows, width), F32), shape((rows, width), BF16)),
        [SMEM] + [VMEM] * 9,
        [VMEM] * 5,
        20 * rows * width * hidden_count,
        0,
    )(place, sib, *weights, *turned, *acc)


def slot_kernel(p, place, *refs):
    write_slots(place, p, *refs)


def slots(place, p, dg, du, turned):
    rows, hidden_count = dg.shape
    width = turned[1].shape[2] // 2
    return call(
        functools.partial(slot_kernel, p),
        (shape((rows, width), F32), shape((rows, width), BF16)),
        [SMEM] + [VMEM] * 4,
        [VMEM] * 2,
        8 * rows * width * hidden_count,
        0,
    )(place, dg, du, *turned)


def weight_kernel(jobs, begun, place, *refs):
    n = len(jobs)
    own, sib, ds = refs[0:4], refs[4:8], refs[8 : 8 + n]
    refs = refs[8 + n + begun :]
    outs, bufs, sems = refs[:n], refs[n : 2 * n], refs[2 * n]
    core = place[0] % 2
    wide = 2 * own[0].shape[2]
    chips = far(place)
    copies = []
    for i, ((array, pieces), d, out, buf) in enumerate(zip(jobs, ds, outs, bufs)):
        for j, p in enumerate(pieces):
            rows = block_at(place, chips[p], wide)
            piece = both_cores(core, own[p][array], sib[p][array])
            left, right = (piece, d[...]) if array == 0 else (d[...], piece)
            size = left.shape[1] // PARTS
            for k in range(PARTS):
                part = pl.ds(k * size, size)
                buf[j, part, :] = dot(left[:, k * size : (k + 1) * size], right, 0, 0).astype(BF16)
                if array == 0:
                    start = pl.multiple_of((place[0] // 2 ^ chips[p]) * wide + k * size, size)
                    target = out.at[pl.ds(start, size), :]
                else:
                    target = out.at[part, rows]
                copies.append(pltpu.make_async_copy(buf.at[j, part, :], target, sems.at[i, j, k]))
                copies[-1].start()
    for copy in copies:
        copy.wait()


def weight_grads(place, jobs, own, sib, ds, begun=None):
    rows, width = own[0].shape[1:]
    hidden_count = ds[0].shape[1]
    blocks = [(2 * width, hidden_count) if array == 0 else (hidden_count, 2 * width) for array, _ in jobs]
    outs = [(8 * width, hidden_count) if array == 0 else (hidden_count, 8 * width) for array, _ in jobs]
    count = sum(len(pieces) for _, pieces in jobs)
    more = [] if begun is None else [begun]
    return call(
        functools.partial(weight_kernel, jobs, len(more)),
        tuple(shape(out, BF16) for out in outs),
        [SMEM] + [VMEM] * (8 + len(ds)) + [HBM] * len(more),
        [HBM] * len(ds),
        4 * rows * width * hidden_count * count,
        4 * width * hidden_count * count,
        scratch=[pltpu.VMEM((len(pieces),) + block, BF16) for block, (_, pieces) in zip(blocks, jobs)]
        + [pltpu.SemaphoreType.DMA((len(ds), 4, PARTS))],
        limit=LOAD_LIMIT,
        aliases={9 + len(ds): 0} if more else {},
    )(place, *own, *sib, *ds, *more)


def pack_kernel(groups, place, *refs):
    sources, outs, here, sems = refs[:4], refs[4 : 4 + groups], refs[4 + groups : 8 + groups], refs[8 + groups]
    copies = [pltpu.make_async_copy(s, d, sems.at[i]) for i, (s, d) in enumerate(zip(sources, here))]
    for copy in copies:
        copy.start()
    for copy in copies:
        copy.wait()
    acts, grad, routing, gates = here
    wide = grad[...].astype(F32)
    for distance, out in enumerate(outs):
        expert = lax.rem(place[0] + distance, groups)
        gate = jnp.sum(jnp.where(routing[...] == expert, gates[...], 0.0), axis=0, keepdims=True)
        out[0] = acts[...]
        out[1] = (wide * gate.T).astype(BF16)


def pack(place, acts, grad, routing, gates, groups):
    sources = tuple(in_hbm(s) for s in (acts, grad, routing.T, gates.T))
    return call(
        functools.partial(pack_kernel, groups),
        (shape((2,) + acts.shape, BF16),) * groups,
        [SMEM] + [HBM] * 4,
        [VMEM] * groups,
        1,
        1,
        scratch=[pltpu.VMEM(s.shape, s.dtype) for s in sources] + [pltpu.SemaphoreType.DMA((4,))],
        limit=16,
    )(place, *sources)


def across(array, even, odd=None):
    masks = (even, even if odd is None else odd)
    return lax.ppermute(array, "tensor", [(i, i ^ masks[i % 2]) for i in range(8)])


def along(array, distance, count):
    return lax.ppermute(array, "expert", [(i, (i + distance) % count) for i in range(count)])


def chips_body(acts, grad_out, routing, gates, w_gate, w_up, w_down):
    groups = lax.axis_size("expert")
    place = lax.axis_index("tensor").astype(jnp.int32)[None]
    z = lax.axis_index("expert").astype(jnp.int32)[None]
    tok_count, width = acts.shape
    packed = pack(z, acts, grad_out, routing, gates, groups)
    blocks = [along(packed[k], k, groups) for k in range(1, groups)]
    wg, wg_turned = load_gate(place, w_gate[0])
    blocks, wg, wg_turned = lax.optimization_barrier((blocks, wg, wg_turned))
    own = jnp.concatenate([packed[0]] + blocks, axis=1)
    near = across(own, 1)
    here = across(own, 2, 4), across(near, 2, 4)
    wu, gate, up, wu_turned = load_up(place, own, near, w_up[0], wg)
    first, gate, up = lax.optimization_barrier((here[0], gate, up))
    diag = across(first, 4, 2)
    there_second = across(first, 1)
    wd = w_down[0]
    back, wd_turned = own_back(place, own, near, wd)
    second, back = lax.optimization_barrier((here[1], back))
    there_first = across(second, 1)
    weights, acc = (wg, wu, wd), (gate, up, back)
    acc = partial_sums(place, first, second, there_second, weights, wd_turned, acc)
    turned = wg_turned, wu_turned
    diag, acc = lax.optimization_barrier((diag, acc))
    diag_near = across(diag, 1)
    acc = third_sums(place, there_first, diag, (wg, wu, wd_turned), acc)
    hid, dg, du, keep, send = middle(place, diag_near, (wg, wu, wd_turned), turned, acc)
    mine_of = own, first, there_first, diag
    other_of = near, second, there_second, diag_near

    def chip_sum(keep, send):
        return keep + across(send, 1).astype(F32)

    shares = {1: slots(place, 1, dg, du, turned)}
    total, dg, du = lax.optimization_barrier((chip_sum(keep, send), dg, du))
    parts = [across(total.astype(BF16), 6)]
    shares[2] = slots(place, 2, dg, du, turned)
    parts.append(across(chip_sum(*shares[1]).astype(BF16), 2))
    total, dg, du = lax.optimization_barrier((chip_sum(*shares[2]), dg, du))
    parts.append(across(total.astype(BF16), 4))
    share = slots(place, 0, dg, du, turned)
    share, dg = lax.optimization_barrier((share, dg))
    (grad_gate,) = weight_grads(place, [(0, (0, 1))], mine_of, other_of, (dg,))
    mine = chip_sum(*share)
    parts[0], dg, grad_gate = lax.optimization_barrier((parts[0], dg, grad_gate))
    (grad_gate,) = weight_grads(place, [(0, (2, 3))], mine_of, other_of, (dg,), grad_gate)
    for part in parts:
        mine = mine + part.astype(F32)
    mine, hid, grad_gate = lax.optimization_barrier((mine, hid, grad_gate))
    whole = (0, 1, 2, 3)
    grad_up, grad_down = weight_grads(place, [(0, whole), (1, whole)], mine_of, other_of, (du, hid))
    mine = mine.reshape(groups, tok_count, width)
    back = mine[0]
    sent = mine.astype(BF16)
    for k in range(1, groups):
        back = back + along(sent[k], -k, groups).astype(F32)
    return (grad_gate[None], grad_up[None], grad_down[None], back.astype(BF16))


def any_body(acts, grad_out, routing, gates, w_gate, w_up, w_down):
    expert = lax.axis_index("expert")
    acts_all, grad_all = (
        lax.all_gather(
            lax.all_gather(array, "tensor", axis=1, tiled=True), "expert", axis=0, tiled=True
        )
        for array in (acts, grad_out)
    )
    routing_all = lax.all_gather(routing, "expert", axis=0, tiled=True)
    gates_all = lax.all_gather(gates, "expert", axis=0, tiled=True)
    grad_all = (grad_all.astype(F32) * gate_of(routing_all, gates_all, expert)).astype(BF16)
    wg, wu, wd = w_gate[0], w_up[0], w_down[0]
    hid, dg, du = hidden_grads(dot(acts_all, wg, 1, 0), dot(acts_all, wu, 1, 0), dot(grad_all, wd, 1, 1))
    partial = dot(dg, wg, 1, 1) + dot(du, wu, 1, 1)
    partial = lax.psum_scatter(partial, "tensor", scatter_dimension=1, tiled=True)
    back = lax.psum_scatter(partial, "expert", scatter_dimension=0, tiled=True)
    return (
        dot(acts_all, dg, 0, 0).astype(BF16)[None],
        dot(acts_all, du, 0, 0).astype(BF16)[None],
        dot(hid, grad_all, 0, 0).astype(BF16)[None],
        back.astype(BF16),
    )


def solution(mesh):
    chips = mesh.shape["tensor"] == 8
    return jax.shard_map(
        chips_body if chips else any_body,
        mesh=mesh,
        in_specs=(
            P("expert", "tensor"),
            P("expert", "tensor"),
            P("expert", None),
            P("expert", None),
            P("expert", None, "tensor"),
            P("expert", None, "tensor"),
            P("expert", "tensor", None),
        ),
        out_specs=(
            P("expert", None, "tensor"),
            P("expert", None, "tensor"),
            P("expert", "tensor", None),
            P("expert", "tensor"),
        ),
        check_vma=False,
    )
```

```python
import functools

import jax
import jax.numpy as jnp
from jax import lax
from jax.experimental import pallas as pl
from jax.experimental.pallas import tpu as pltpu
from jax.sharding import PartitionSpec as P

F32 = jnp.float32
BF16 = jnp.bfloat16


def dot(left, right, left_dim, right_dim):
    return lax.dot_general(
        left, right, (((left_dim,), (right_dim,)), ((), ())), preferred_element_type=F32
    )


def gate_of(routing, gates, expert):
    return jnp.sum(jnp.where(routing == expert, gates, 0.0), axis=1, keepdims=True)


def hidden_grads(gate_pre, up_pre, grad_hidden):
    sig = jax.nn.sigmoid(gate_pre)
    act = gate_pre * sig
    hidden = (act * up_pre).astype(BF16)
    grad_up_pre = (grad_hidden * act).astype(BF16)
    grad_gate_pre = (grad_hidden * up_pre * sig * (1.0 + gate_pre * (1.0 - sig))).astype(BF16)
    return hidden, grad_gate_pre, grad_up_pre


VMEM = pl.BlockSpec(memory_space=pltpu.VMEM)
SMEM = pl.BlockSpec(memory_space=pltpu.SMEM)
HBM = pl.BlockSpec(memory_space=pl.ANY)


def in_hbm(array):
    return pltpu.with_memory_space_constraint(array, pltpu.HBM)


def shape(dims, dtype):
    return jax.ShapeDtypeStruct(dims, dtype)


def call(kernel, out_shape, in_specs, out_specs, flops, moved, scratch=(), limit=8, aliases={}):
    return pl.pallas_call(
        kernel,
        out_shape=out_shape,
        in_specs=in_specs,
        out_specs=out_specs,
        scratch_shapes=scratch,
        input_output_aliases=aliases,
        compiler_params=pltpu.CompilerParams(vmem_limit_bytes=limit * 1024 * 1024),
        cost_estimate=pl.CostEstimate(flops=flops, bytes_accessed=moved, transcendentals=0),
    )


def both_cores(core, mine, other):
    first = core == 0
    return jnp.concatenate([jnp.where(first, mine, other), jnp.where(first, other, mine)], axis=1)


def block_at(place, p, wide):
    return pl.ds(pl.multiple_of((place[0] // 2 ^ p) * wide, wide), wide)


STEP = 256
LOAD_LIMIT = 18
PARTS = 2


def far(place):
    core = place[0] % 2
    return 0, 1 + core, 2 - core, 3


def pair(place, i, own, sib):
    core = place[0] % 2
    rows = block_at(place, far(place)[i], 2 * own.shape[2])
    return rows, both_cores(core, own[0], sib[0]), both_cores(core, own[1], sib[1])


def add_pieces(pieces, weights, acc_in, acc_out, finish):
    wg, wu, wd = weights
    for f in range(wg.shape[1] // STEP):
        cols = pl.ds(f * STEP, STEP)
        sums = [None if acc is None else acc[:, cols] for acc in acc_in]
        for rows, x, g in pieces:
            terms = (dot(x, wg[rows, cols], 1, 0), dot(x, wu[rows, cols], 1, 0), dot(g, wd[cols, rows], 1, 1))
            sums = [t if s is None else s + t for s, t in zip(sums, terms)]
        finish(cols, sums, acc_out)


def store(cols, sums, outs):
    for out, value in zip(outs, sums):
        out[:, cols] = value


def store_grads(cols, sums, outs):
    store(cols, hidden_grads(*sums), outs)


def turn(block, out):
    for c in range(0, block.shape[1], STEP):
        out[c : c + STEP, :] = block[:, c : c + STEP].T


def load_gate_kernel(place, source, here, turned, sems):
    wide = turned.shape[2]
    blocks = [block_at(place, p, wide) for p in range(4)]
    copies = [pltpu.make_async_copy(source.at[b, :], here.at[b, :], sems.at[p]) for p, b in enumerate(blocks)]
    for copy in copies:
        copy.start()
    for p, block in enumerate(blocks):
        copies[p].wait()
        turn(here[block, :], turned.at[p])


def load_gate(place, wg):
    full, hidden_count = wg.shape
    return call(
        load_gate_kernel,
        (shape(wg.shape, BF16), shape((4, hidden_count, full // 4), BF16)),
        [SMEM, HBM],
        [VMEM] * 2,
        1,
        1,
        scratch=[pltpu.SemaphoreType.DMA((4,))],
        limit=8,
    )(place, in_hbm(wg))


def load_up_kernel(place, own, near, source, wg, here, gate, up, turned, sems):
    row, x, _ = pair(place, 0, own, near)
    wide = x.shape[1]
    copies = []
    for p in range(4):
        rows = block_at(place, p, wide)
        copies.append(pltpu.make_async_copy(source.at[rows, :], here.at[rows, :], sems.at[p]))
        copies[p].start()
    for weight, total in ((wg, gate), (here, up)):
        if weight is here:
            copies[0].wait()
        for f in range(weight.shape[1] // STEP):
            cols = pl.ds(f * STEP, STEP)
            total[:, cols] = dot(x, weight[row, cols], 1, 0)
    for p in range(4):
        if p > 0:
            copies[p].wait()
        turn(here[block_at(place, p, wide), :], turned.at[p])


def load_up(place, own, near, wu, wg):
    rows, hidden_count = own.shape[1], wu.shape[1]
    return call(
        load_up_kernel,
        (shape(wu.shape, BF16),)
        + (shape((rows, hidden_count), F32),) * 2
        + (shape((4, hidden_count, wu.shape[0] // 4), BF16),),
        [SMEM] + [VMEM] * 2 + [HBM] + [VMEM],
        [VMEM] * 4,
        1,
        1,
        scratch=[pltpu.SemaphoreType.DMA((4,))],
        limit=8,
    )(place, own, near, in_hbm(wu), wg)


def back_kernel(place, own, near, wd, back, turned):
    row, _, g = pair(place, 0, own, near)
    for f in range(wd.shape[0] // STEP):
        cols = pl.ds(f * STEP, STEP)
        back[:, cols] = dot(g, wd[cols, row], 1, 1)
        for i in range(2):
            turned[i, :, cols] = wd[cols, block_at(place, far(place)[2 + i], g.shape[1])].T


def own_back(place, own, near, wd):
    rows, (hidden_count, full) = own.shape[1], wd.shape
    return call(
        back_kernel,
        (shape((rows, hidden_count), F32), shape((2, full // 4, hidden_count), BF16)),
        [SMEM] + [VMEM] * 3,
        [VMEM] * 2,
        1,
        1,
    )(place, own, near, wd)


def half_at(place, i, core, half, wg, wu, turned):
    x, g = half[0], half[1]
    width = x.shape[1]
    rows = (place[0] // 2 ^ far(place)[i]) * 2 * width + core * width
    rows = pl.ds(pl.multiple_of(rows, width), width)
    down = pl.ds(pl.multiple_of(core * width, width), width)

    def terms(cols):
        return dot(x, wg[rows, cols], 1, 0), dot(x, wu[rows, cols], 1, 0), dot(g, turned[i - 2, down, cols], 1, 0)

    return terms


def add_halves(halves, count, acc_in, finish, acc_out):
    for f in range(count // STEP):
        cols = pl.ds(f * STEP, STEP)
        sums = [acc[:, cols] for acc in acc_in]
        for terms in halves:
            sums = [s + t for s, t in zip(sums, terms(cols))]
        finish(cols, sums, acc_out)


def partial_kernel(place, own, sib, other, wg, wu, wd, turned, *refs):
    add_pieces([pair(place, 1, own, sib)], (wg, wu, wd), refs[:3], refs[3:], store)
    terms = half_at(place, 2, 1 - place[0] % 2, other, wg, wu, turned)
    add_halves([terms], wg.shape[1], refs[3:], store, refs[3:])


def partial_sums(place, own, sib, other, weights, turned, acc):
    return call(
        partial_kernel,
        (shape(acc[0].shape, F32),) * 3,
        [SMEM] + [VMEM] * 10,
        [VMEM] * 3,
        1,
        1,
        aliases={8: 0, 9: 1, 10: 2},
    )(place, own, sib, other, *weights, turned, *acc)


def third_kernel(place, rest, diag, wg, wu, turned, *refs):
    core = place[0] % 2
    halves = [half_at(place, i, core, half, wg, wu, turned) for i, half in ((2, rest), (3, diag))]
    add_halves(halves, wg.shape[1], refs[:3], store, refs[3:])


def third_sums(place, rest, diag, weights, acc):
    return call(
        third_kernel,
        (shape(acc[0].shape, F32),) * 3,
        [SMEM] + [VMEM] * 8,
        [VMEM] * 3,
        1,
        1,
        aliases={6: 0, 7: 1, 8: 2},
    )(place, rest, diag, *weights, *acc)


def write_slots(place, p, dg, du, wg, wu, keep, send):
    width = keep.shape[1]
    first = place[0] % 2 == 0
    part = dot(dg[...], wg[p], 1, 0) + dot(du[...], wu[p], 1, 0)
    low, high = part[:, :width], part[:, width:]
    keep[...] = jnp.where(first, low, high)
    send[...] = jnp.where(first, high, low).astype(BF16)


def middle_kernel(place, sib, wg, wu, turned, wg_turned, wu_turned, gate, up, back, hid, dg, du, keep, send):
    terms = half_at(place, 3, 1 - place[0] % 2, sib, wg, wu, turned)
    add_halves([terms], wg.shape[1], (gate, up, back), store_grads, (hid, dg, du))
    write_slots(place, 3, dg, du, wg_turned, wu_turned, keep, send)


def middle(place, sib, weights, turned, acc):
    rows, width = sib.shape[1:]
    hidden_count = turned[0].shape[1]
    return call(
        middle_kernel,
        (shape((rows, hidden_count), BF16),) * 3 + (shape((rows, width), F32), shape((rows, width), BF16)),
        [SMEM] + [VMEM] * 9,
        [VMEM] * 5,
        20 * rows * width * hidden_count,
        0,
    )(place, sib, *weights, *turned, *acc)


def slot_kernel(p, place, *refs):
    write_slots(place, p, *refs)


def slots(place, p, dg, du, turned):
    rows, hidden_count = dg.shape
    width = turned[1].shape[2] // 2
    return call(
        functools.partial(slot_kernel, p),
        (shape((rows, width), F32), shape((rows, width), BF16)),
        [SMEM] + [VMEM] * 4,
        [VMEM] * 2,
        8 * rows * width * hidden_count,
        0,
    )(place, dg, du, *turned)


def weight_kernel(jobs, begun, place, *refs):
    n = len(jobs)
    own, sib, ds = refs[0:4], refs[4:8], refs[8 : 8 + n]
    refs = refs[8 + n + begun :]
    outs, bufs, sems = refs[:n], refs[n : 2 * n], refs[2 * n]
    core = place[0] % 2
    wide = 2 * own[0].shape[2]
    chips = far(place)
    copies = []
    for i, ((array, pieces), d, out, buf) in enumerate(zip(jobs, ds, outs, bufs)):
        for j, p in enumerate(pieces):
            rows = block_at(place, chips[p], wide)
            piece = both_cores(core, own[p][array], sib[p][array])
            left, right = (piece, d[...]) if array == 0 else (d[...], piece)
            size = left.shape[1] // PARTS
            for k in range(PARTS):
                part = pl.ds(k * size, size)
                buf[j, part, :] = dot(left[:, k * size : (k + 1) * size], right, 0, 0).astype(BF16)
                if array == 0:
                    start = pl.multiple_of((place[0] // 2 ^ chips[p]) * wide + k * size, size)
                    target = out.at[pl.ds(start, size), :]
                else:
                    target = out.at[part, rows]
                copies.append(pltpu.make_async_copy(buf.at[j, part, :], target, sems.at[i, j, k]))
                copies[-1].start()
    for copy in copies:
        copy.wait()


def weight_grads(place, jobs, own, sib, ds, begun=None):
    rows, width = own[0].shape[1:]
    hidden_count = ds[0].shape[1]
    blocks = [(2 * width, hidden_count) if array == 0 else (hidden_count, 2 * width) for array, _ in jobs]
    outs = [(8 * width, hidden_count) if array == 0 else (hidden_count, 8 * width) for array, _ in jobs]
    count = sum(len(pieces) for _, pieces in jobs)
    more = [] if begun is None else [begun]
    return call(
        functools.partial(weight_kernel, jobs, len(more)),
        tuple(shape(out, BF16) for out in outs),
        [SMEM] + [VMEM] * (8 + len(ds)) + [HBM] * len(more),
        [HBM] * len(ds),
        4 * rows * width * hidden_count * count,
        4 * width * hidden_count * count,
        scratch=[pltpu.VMEM((len(pieces),) + block, BF16) for block, (_, pieces) in zip(blocks, jobs)]
        + [pltpu.SemaphoreType.DMA((len(ds), 4, PARTS))],
        limit=LOAD_LIMIT,
        aliases={9 + len(ds): 0} if more else {},
    )(place, *own, *sib, *ds, *more)


def pack_kernel(groups, place, *refs):
    sources, outs, here, sems = refs[:4], refs[4 : 4 + groups], refs[4 + groups : 8 + groups], refs[8 + groups]
    copies = [pltpu.make_async_copy(s, d, sems.at[i]) for i, (s, d) in enumerate(zip(sources, here))]
    for copy in copies:
        copy.start()
    for copy in copies:
        copy.wait()
    acts, grad, routing, gates = here
    wide = grad[...].astype(F32)
    for distance, out in enumerate(outs):
        expert = lax.rem(place[0] + distance, groups)
        gate = jnp.sum(jnp.where(routing[...] == expert, gates[...], 0.0), axis=0, keepdims=True)
        out[0] = acts[...]
        out[1] = (wide * gate.T).astype(BF16)


def pack(place, acts, grad, routing, gates, groups):
    sources = tuple(in_hbm(s) for s in (acts, grad, routing.T, gates.T))
    return call(
        functools.partial(pack_kernel, groups),
        (shape((2,) + acts.shape, BF16),) * groups,
        [SMEM] + [HBM] * 4,
        [VMEM] * groups,
        1,
        1,
        scratch=[pltpu.VMEM(s.shape, s.dtype) for s in sources] + [pltpu.SemaphoreType.DMA((4,))],
        limit=16,
    )(place, *sources)


def across(array, even, odd=None):
    masks = (even, even if odd is None else odd)
    return lax.ppermute(array, "tensor", [(i, i ^ masks[i % 2]) for i in range(8)])


def along(array, distance, count):
    return lax.ppermute(array, "expert", [(i, (i + distance) % count) for i in range(count)])


def chips_body(acts, grad_out, routing, gates, w_gate, w_up, w_down):
    groups = lax.axis_size("expert")
    place = lax.axis_index("tensor").astype(jnp.int32)[None]
    z = lax.axis_index("expert").astype(jnp.int32)[None]
    tok_count, width = acts.shape
    packed = pack(z, acts, grad_out, routing, gates, groups)
    blocks = [along(packed[k], k, groups) for k in range(1, groups)]
    wg, wg_turned = load_gate(place, w_gate[0])
    blocks, wg, wg_turned = lax.optimization_barrier((blocks, wg, wg_turned))
    own = jnp.concatenate([packed[0]] + blocks, axis=1)
    near = across(own, 1)
    here = across(own, 2, 4), across(near, 2, 4)
    wu, gate, up, wu_turned = load_up(place, own, near, w_up[0], wg)
    first, gate, up = lax.optimization_barrier((here[0], gate, up))
    diag = across(first, 4, 2)
    there_second = across(first, 1)
    wd = w_down[0]
    back, wd_turned = own_back(place, own, near, wd)
    second, back = lax.optimization_barrier((here[1], back))
    there_first = across(second, 1)
    weights, acc = (wg, wu, wd), (gate, up, back)
    acc = partial_sums(place, first, second, there_second, weights, wd_turned, acc)
    turned = wg_turned, wu_turned
    diag, acc = lax.optimization_barrier((diag, acc))
    diag_near = across(diag, 1)
    acc = third_sums(place, there_first, diag, (wg, wu, wd_turned), acc)
    hid, dg, du, keep, send = middle(place, diag_near, (wg, wu, wd_turned), turned, acc)
    mine_of = own, first, there_first, diag
    other_of = near, second, there_second, diag_near

    def chip_sum(keep, send):
        return keep + across(send, 1).astype(F32)

    shares = {1: slots(place, 1, dg, du, turned)}
    total, dg, du = lax.optimization_barrier((chip_sum(keep, send), dg, du))
    parts = [across(total.astype(BF16), 6)]
    shares[2] = slots(place, 2, dg, du, turned)
    parts.append(across(chip_sum(*shares[1]).astype(BF16), 2))
    total, dg, du = lax.optimization_barrier((chip_sum(*shares[2]), dg, du))
    parts.append(across(total.astype(BF16), 4))
    share = slots(place, 0, dg, du, turned)
    share, dg = lax.optimization_barrier((share, dg))
    (grad_gate,) = weight_grads(place, [(0, (0, 1))], mine_of, other_of, (dg,))
    mine = chip_sum(*share)
    parts[0], dg, grad_gate = lax.optimization_barrier((parts[0], dg, grad_gate))
    (grad_gate,) = weight_grads(place, [(0, (2,))], mine_of, other_of, (dg,), grad_gate)
    for part in parts:
        mine = mine + part.astype(F32)
    mine, hid, grad_gate = lax.optimization_barrier((mine, hid, grad_gate))
    whole = (0, 1, 2, 3)
    jobs = [(0, (3,)), (0, whole), (1, whole)]
    grad_gate, grad_up, grad_down = weight_grads(place, jobs, mine_of, other_of, (dg, du, hid), grad_gate)
    mine = mine.reshape(groups, tok_count, width)
    back = mine[0]
    sent = mine.astype(BF16)
    for k in range(1, groups):
        back = back + along(sent[k], -k, groups).astype(F32)
    return (grad_gate[None], grad_up[None], grad_down[None], back.astype(BF16))


def any_body(acts, grad_out, routing, gates, w_gate, w_up, w_down):
    expert = lax.axis_index("expert")
    acts_all, grad_all = (
        lax.all_gather(
            lax.all_gather(array, "tensor", axis=1, tiled=True), "expert", axis=0, tiled=True
        )
        for array in (acts, grad_out)
    )
    routing_all = lax.all_gather(routing, "expert", axis=0, tiled=True)
    gates_all = lax.all_gather(gates, "expert", axis=0, tiled=True)
    grad_all = (grad_all.astype(F32) * gate_of(routing_all, gates_all, expert)).astype(BF16)
    wg, wu, wd = w_gate[0], w_up[0], w_down[0]
    hid, dg, du = hidden_grads(dot(acts_all, wg, 1, 0), dot(acts_all, wu, 1, 0), dot(grad_all, wd, 1, 1))
    partial = dot(dg, wg, 1, 1) + dot(du, wu, 1, 1)
    partial = lax.psum_scatter(partial, "tensor", scatter_dimension=1, tiled=True)
    back = lax.psum_scatter(partial, "expert", scatter_dimension=0, tiled=True)
    return (
        dot(acts_all, dg, 0, 0).astype(BF16)[None],
        dot(acts_all, du, 0, 0).astype(BF16)[None],
        dot(hid, grad_all, 0, 0).astype(BF16)[None],
        back.astype(BF16),
    )


def solution(mesh):
    chips = mesh.shape["tensor"] == 8
    return jax.shard_map(
        chips_body if chips else any_body,
        mesh=mesh,
        in_specs=(
            P("expert", "tensor"),
            P("expert", "tensor"),
            P("expert", None),
            P("expert", None),
            P("expert", None, "tensor"),
            P("expert", None, "tensor"),
            P("expert", "tensor", None),
        ),
        out_specs=(
            P("expert", None, "tensor"),
            P("expert", None, "tensor"),
            P("expert", "tensor", None),
            P("expert", "tensor"),
        ),
        check_vma=False,
    )
```
